256 devices in a mesh: rep: 8 (over x, y_lo), ep: 32 (over y_hi, z, core).
Axes of the slice: x: 4, y: 4 (y_hi: 2, y_lo: 2; y = y_hi * 2 + y_lo), z: 8, core: 2. Of those that a mesh axis runs over, the one named last changes fastest.
Arguments:
- hidden_in: bfloat16 [4, 64, 7168], P(None, 'ep'), may hold values from -6 to 6
- queries: bfloat16 [4, 64, 8192], P(None, None, 'ep'), may hold values from -216 to 216
- new_keys: bfloat16 [4, 64, 8192], P(None, None, 'ep'), may hold values from -6 to 6
- new_values: bfloat16 [4, 64, 8192], P(None, None, 'ep'), may hold values from -6 to 6
- cache_keys: bfloat16 [64, 32, 8192], P(None, None, 'ep'), may hold values from -6 to 6
- cache_values: bfloat16 [64, 32, 8192], P(None, None, 'ep'), may hold values from -6 to 6
- cache_lengths: int32 [64], replicated, may hold values from 1 to 32, 1056 in all
- expert_ids: int32 [4, 64, 8], P(None, 'ep'), may hold values from 0 to 31, all different within a row; in each aligned block of 2 rows (0 to 1, 2 to 3, ..., all dimensions but the last counted through in order) at most 2 rows name the same one
- router_logits: float32 [4, 64, 8], P(None, 'ep'), may hold values from -6 to 6
- norm_gain: float32 [7168], replicated, may hold values from 0.1 to 1.9
- out_sectioned: bfloat16 [8192, 7168], P('ep', 'rep'), may hold values from -0.0625 to 0.0625
- expert_sectioned: bfloat16 [32, 7168, 3, 1024], P('ep', 'rep'), may hold values from -0.09375 to 0.09375
- bucket_owner: int32 [32, 8], P('ep'), may hold values from 0 to 7, each once within a row
Outputs:
- layer_out: bfloat16 [4, 64, 7168], P(None, 'ep')
The draws below stay inside these ranges and needn't reach their ends.
Inputs may be any that keep to these rules, and one draw needn't show every extreme that they name: `expert_ids`: within one step, the rows of one device (aligned blocks of 2 rows) name no expert more than 2 times; some expert is named exactly 2 times. Each row names distinct experts. `bucket_owner`: for each expert the owners of its 8 buckets are distinct.
All inputs are finite; a program needn't handle non-finite values.
Results may differ from the reference program's by a relative error of at most 0.025.
Values may be sent and summed in bfloat16 or wider, within the bound.
No kernel may reach another device: no remote copies, remote signals or barrier semaphores. Data moves between devices by JAX's collectives and lax.ppermute only.
A program may use at most 128 MiB of HBM per device.

```python
import math
import jax
import jax.numpy as jnp
import numpy as np
from jax import lax

D = 7168
H = 64
DH = 128
FFE = 1024
TOPK = 8
STEPS = 4
ROWS = 64
CACHE = 32
EXPERTS = 32
CAP = 2
N_REP = 8
N_EP = 32


def shared_keys(key):
    return jnp.clip(jax.random.normal(key, (ROWS, CACHE, H * DH), jnp.float32), -6.0, 6.0)


def draw_cache_keys(key, part):
    base = shared_keys(key)
    return base.astype(jnp.bfloat16)


def draw_queries(key, part):
    key = jax.random.fold_in(key, 7)
    fresh = jnp.clip(jax.random.normal(key, (STEPS, ROWS, H * DH), jnp.float32), -6.0, 6.0)
    return fresh.astype(jnp.bfloat16)


def level_of(rng, shape, cuts, low, high):
    loudness = 1.0
    for position, parts in cuts:
        steps = jax.random.uniform(jax.random.fold_in(jax.random.fold_in(rng, 6), position), (parts,), jnp.float32, low / len(cuts), high / len(cuts))
        loudness = loudness * jnp.repeat(jnp.exp(steps), shape[position] // parts).reshape((-1,) + (1,) * (len(shape) - 1 - position))
    return loudness


def split_up(count, total, bound, slope):
    loads = [(1 << 20) // math.isqrt(grade ** slope) + 1 for grade in range(2, count + 1)]
    spare, counts = total - bound - (count - 1), [1] * (count - 1)
    while spare > 0:
        candidates = [i for i in range(count - 1) if counts[i] < bound]
        whole, budget = sum([loads[i] for i in candidates]), spare
        for i in candidates:
            more = min(bound - counts[i], max(1, budget * loads[i] // whole), spare)
            counts[i] = counts[i] + more
            spare = spare - more
    return np.array([bound] + counts)


def ragged(rng, amount, total, limit, slope):
    if amount == 2:
        one = jax.random.randint(rng, (), max(1, total - limit), min(limit, total - 1) + 1)
        return jnp.stack([one, total - one])
    lengths = jnp.asarray(split_up(amount, total, limit, slope), jnp.int32)
    twos = (amount - 1) // 2
    source_of, sink = lengths[1:1 + 2 * twos:2], lengths[2:2 + 2 * twos:2]
    slack = jnp.minimum(source_of - 1, limit - sink)
    passed = jax.random.randint(jax.random.fold_in(rng, 1), (twos,), 0, 1 << 20) % (slack + 1)
    lengths = lengths.at[1:1 + 2 * twos:2].set(source_of - passed).at[2:2 + 2 * twos:2].set(sink + passed)
    return lengths[jax.random.permutation(jax.random.fold_in(rng, 2), amount)]


def assign_block(rng, own, number, rows, amount, top, reach, skew):
    sequence = jax.random.permutation(rng, amount)
    heavy_load, common = portions_of(amount, rows * top, reach, skew, True), portions_of(amount, rows * top, reach, skew, False)
    places = jnp.arange(amount)

    def named(lengths, turn):
        used = int((lengths > 0).sum())
        fixed = max(1, used // 4)
        moved = fixed + (places - fixed + turn * (used - fixed)) % max(1, amount - fixed)
        return jnp.zeros((amount,), jnp.int32).at[sequence[jnp.where(places < fixed, places, moved)]].set(jnp.asarray(lengths, jnp.int32))

    lengths = jnp.where(number % 4 == 0, named(heavy_load, number // 4), named(common, number - number // 4 - 1))
    mixed = jax.random.permutation(jax.random.fold_in(own, 3), amount)
    source_of, receiver = mixed[0:amount // 2 * 2:2], mixed[1:amount // 2 * 2:2]
    margin = jnp.minimum(lengths[source_of] - 1, reach - lengths[receiver]) // 2
    margin = jnp.where((source_of == sequence[0]) | (receiver == sequence[0]) | (lengths[receiver] == 0), 0, jnp.maximum(margin, 0))
    moved = jax.random.randint(jax.random.fold_in(own, 4), (amount // 2,), 0, 1 << 20) % (margin + 1)
    lengths = lengths.at[source_of].add(-moved).at[receiver].add(moved)
    items = jnp.searchsorted(jnp.cumsum(lengths), jnp.arange(rows * top), side="right").astype(jnp.int32)
    grid = items.reshape(top, rows).T
    grid = grid[jax.random.permutation(jax.random.fold_in(own, 1), rows)]
    turn = jax.random.randint(jax.random.fold_in(own, 2), (rows, 1), 0, top)
    return jnp.take_along_axis(grid, (jnp.arange(top)[None, :] + turn) % top, axis=1)


def portions_of(count, total, bound, skew, full):
    loads = [(1 << 20) // math.isqrt(rank ** skew) + 1 for rank in range(1, count + 1)]
    largest = bound if full else min(bound, max(-(-total // count), total * loads[0] // sum(loads)))
    least = 1 if total - largest >= count - 1 else 0
    counts, spare = [largest] + [least] * (count - 1), total - largest - least * (count - 1)
    while spare > 0:
        movable = [i for i in range(1, count) if counts[i] < largest] or [i for i in range(1, count) if counts[i] < bound]
        pool, remaining = sum([loads[i] for i in movable]), spare
        for i in movable:
            addition = min(bound - counts[i], max(1, remaining * loads[i] // pool), spare)
            counts[i] = counts[i] + addition
            spare = spare - addition
    return np.array(counts)


def gaussian(key, shape, deviation, most, cuts=(), kind=jnp.bfloat16):
    gain = level_of(key, shape, cuts, -0.22, 0.18) if cuts else 1.0
    values = jax.random.normal(key, shape, jnp.float32) * deviation * gain
    return jnp.minimum(jnp.maximum(values, -most), most).astype(kind)


def setup_inputs(seed: int = 0) -> dict:
    splits = jax.random.split(jax.random.key(seed), 14)
    hidden_in = gaussian(splits[0], (STEPS, ROWS, D), 1.0, 6.0, ((1, 32),))
    queries = draw_queries(jax.random.fold_in(splits[13], 71), 0)
    new_keys = gaussian(splits[2], (STEPS, ROWS, H * DH), 1.0, 6.0, ((2, 32),))
    new_values = gaussian(splits[3], (STEPS, ROWS, H * DH), 1.0, 6.0, ((2, 32),))
    cache_keys = draw_cache_keys(jax.random.fold_in(splits[13], 71), 0)
    cache_values = gaussian(splits[5], (ROWS, CACHE, H * DH), 1.0, 6.0, ((2, 32),))
    cache_lengths = ragged(splits[6], ROWS, ROWS * (CACHE + 1) // 2, CACHE, 1).astype(jnp.int32)
    expert_ids_keys = jax.random.split(jax.random.fold_in(splits[7], 1), STEPS * ROWS // (ROWS // N_EP))
    expert_ids_turns = jax.random.permutation(jax.random.fold_in(splits[7], 3), STEPS * ROWS // (ROWS // N_EP))
    expert_ids = jax.vmap(lambda own, number: assign_block(jax.random.fold_in(splits[7], 2), own, number, ROWS // N_EP, EXPERTS, TOPK, CAP, 2))(expert_ids_keys, expert_ids_turns).reshape((STEPS, ROWS, TOPK))
    router_logits = gaussian(splits[8], (STEPS, ROWS, TOPK), 1.5, 6.0, ((1, 32),), jnp.float32)
    norm_gain = jnp.clip(1.0 + 0.18 * jax.random.normal(splits[9], (D,), jnp.float32), 0.1, 1.9)
    out_sectioned = gaussian(splits[10], (H * DH, D), (H * DH) ** -0.5, 0.0625, ((0, 32), (1, 8)))
    expert_sectioned = gaussian(splits[11], (EXPERTS, D, 3, FFE), (D // 2) ** -0.5, 0.09375, ((0, 32), (1, 8)))
    bucket_owner = jax.vmap(lambda own: jax.random.permutation(own, N_REP))(jax.random.split(splits[12], EXPERTS)).reshape((EXPERTS, N_REP)).astype(jnp.int32)
    return {"hidden_in": hidden_in, "queries": queries, "new_keys": new_keys, "new_values": new_values, "cache_keys": cache_keys, "cache_values": cache_values, "cache_lengths": cache_lengths, "expert_ids": expert_ids, "router_logits": router_logits, "norm_gain": norm_gain, "out_sectioned": out_sectioned, "expert_sectioned": expert_sectioned, "bucket_owner": bucket_owner}


ROUTE_SCALE = 2.827
EPSILON = 1e-06

def attention(query_rows, key_cache, value_cache, fresh_keys, fresh_values, row_lengths, step_index):
    row_count, feature_count = query_rows.shape
    head_count = feature_count // DH
    cached = key_cache.shape[1]
    step_count = fresh_keys.shape[0]
    query_heads = query_rows.reshape(row_count, head_count, DH).astype(jnp.float32)
    keys_old = key_cache.reshape(row_count, cached, head_count, DH).astype(jnp.float32)
    values_old = value_cache.reshape(row_count, cached, head_count, DH).astype(jnp.float32)
    keys_recent = fresh_keys.reshape(step_count, row_count, head_count, DH).astype(jnp.float32)
    values_recent = fresh_values.reshape(step_count, row_count, head_count, DH).astype(jnp.float32)
    factor = 1.0 / math.sqrt(DH)
    scores_old = jnp.einsum('rhd,rchd->rhc', query_heads, keys_old) * factor
    in_cache = jnp.arange(cached, dtype=jnp.int32)[None, :] < row_lengths[:, None]
    scores_old = jnp.where(in_cache[:, None, :], scores_old, -1e+30)
    scores_recent = jnp.einsum('rhd,srhd->rhs', query_heads, keys_recent) * factor
    visible = jnp.arange(step_count, dtype=jnp.int32) <= step_index
    scores_recent = jnp.where(visible[None, None, :], scores_recent, -1e+30)
    scores = jnp.concatenate([scores_old, scores_recent], axis=2)
    largest = lax.optimization_barrier(jnp.max(scores, axis=2, keepdims=True))
    expsum = jnp.exp(scores - largest)
    denominator = lax.optimization_barrier(jnp.sum(expsum, axis=2))
    probs = lax.optimization_barrier(expsum.astype(jnp.bfloat16)).astype(jnp.float32)
    weighted = jnp.einsum('rhc,rchd->rhd', probs[:, :, :cached], values_old)
    weighted = weighted + jnp.einsum('rhs,srhd->rhd', probs[:, :, cached:], values_recent)
    return (weighted / denominator[:, :, None]).astype(jnp.bfloat16).reshape(row_count, feature_count)

def reference(hidden_in, queries, new_keys, new_values, cache_keys, cache_values, cache_lengths, expert_ids, router_logits, norm_gain, out_sectioned, expert_sectioned, bucket_owner):
    head_list = [attention(queries[step_index], cache_keys, cache_values, new_keys, new_values, cache_lengths, step_index) for step_index in range(STEPS)]
    head_matrix = jnp.stack(head_list).reshape(STEPS * ROWS, H * DH)
    group_width = H * DH // N_EP

    def add_group(running, offset):
        rows_part = lax.dynamic_slice_in_dim(head_matrix, offset, group_width, 1)
        weight_part = lax.dynamic_slice_in_dim(out_sectioned, offset, group_width, 0)
        term = jnp.dot(rows_part, weight_part, preferred_element_type=jnp.float32)
        rounded = lax.optimization_barrier(term.astype(jnp.bfloat16))
        return (running + rounded.astype(jnp.float32), None)
    offsets = (jnp.arange(N_EP, dtype=jnp.int32) * group_width).astype(jnp.int32)
    summed, unused = lax.scan(add_group, jnp.zeros((STEPS * ROWS, D), jnp.float32), offsets)
    attended = summed.astype(jnp.bfloat16).reshape(STEPS, ROWS, D)
    residual = hidden_in.astype(jnp.float32) + attended.astype(jnp.float32)
    mean_square = lax.optimization_barrier(jnp.mean(residual * residual, axis=2, keepdims=True))
    normalized = (residual * lax.rsqrt(mean_square + EPSILON) * norm_gain).astype(jnp.bfloat16)
    row_block = ROWS // N_EP
    chosen = expert_ids.reshape(STEPS, N_EP, row_block * TOPK)
    one_hot = (chosen[..., None] == jnp.arange(EXPERTS, dtype=jnp.int32)).astype(jnp.int32)
    earlier_count = lax.optimization_barrier(jnp.sum((jnp.cumsum(one_hot, axis=2) - one_hot) * one_hot, axis=3))
    per_expert = N_EP * STEPS * CAP
    device_offset = jnp.arange(N_EP, dtype=jnp.int32)[None, :, None] * (STEPS * CAP)
    step_offset = jnp.arange(STEPS, dtype=jnp.int32)[:, None, None] * CAP
    slot_order = (chosen * per_expert + device_offset + step_offset + earlier_count).reshape(-1).astype(jnp.int32)
    repeated = jnp.repeat(normalized.reshape(STEPS * ROWS, D), TOPK, axis=0)
    buffer_rows = jnp.zeros((EXPERTS * per_expert, D), jnp.bfloat16).at[slot_order].set(repeated)

    def expert_output(operands):
        block_rows, sectioned, owners = operands
        row_blocks = sectioned.reshape(N_REP, D // N_REP, 3, FFE)
        weight = jnp.take(row_blocks, owners, axis=0).reshape(D, 3, FFE)
        gate_value = jnp.dot(block_rows, weight[:, 0], preferred_element_type=jnp.float32)
        up_value = jnp.dot(block_rows, weight[:, 1], preferred_element_type=jnp.float32)
        activated = (jax.nn.silu(gate_value) * up_value).astype(jnp.bfloat16)
        return jnp.dot(activated, weight[:, 2].T, preferred_element_type=jnp.float32).astype(jnp.bfloat16)
    outputs = lax.map(expert_output, (buffer_rows.reshape(EXPERTS, per_expert, D), expert_sectioned, bucket_owner))
    picked = outputs.reshape(EXPERTS * per_expert, D)[slot_order].astype(jnp.float32).reshape(STEPS, ROWS, TOPK, D)
    affinity = jax.nn.sigmoid(router_logits)
    gate_share = ROUTE_SCALE * affinity / lax.optimization_barrier(jnp.sum(affinity, axis=2, keepdims=True))
    routed = lax.optimization_barrier(jnp.sum(gate_share[..., None] * picked, axis=2))
    return (residual + routed).astype(jnp.bfloat16)
```

```python
import math

import jax
import jax.numpy as jnp
from jax import lax
from jax.sharding import PartitionSpec as P

DH = 128
ROUTE_SCALE = 2.827
EPSILON = 1e-06


def attention(queries, cache_keys, cache_values, new_keys, new_values, lengths):
    steps, rows, width = queries.shape
    heads = width // DH
    cached = cache_keys.shape[1]
    q = queries.reshape(steps, rows, heads, DH)
    ko = cache_keys.reshape(rows, cached, heads, DH)
    vo = cache_values.reshape(rows, cached, heads, DH)
    kn = new_keys.reshape(steps, rows, heads, DH)
    vn = new_values.reshape(steps, rows, heads, DH)
    factor = 1.0 / math.sqrt(DH)
    so = jnp.einsum("trhd,rchd->rhtc", q, ko, preferred_element_type=jnp.float32) * factor
    sn = jnp.einsum("trhd,srhd->rhts", q, kn, preferred_element_type=jnp.float32) * factor
    live = jnp.arange(cached, dtype=jnp.int32)[None, :] < lengths[:, None]
    so = jnp.where(live[:, None, None, :], so, -1e30)
    order = jnp.arange(steps, dtype=jnp.int32)
    sn = jnp.where(order[None, :] <= order[:, None], sn, -1e30)
    scores = jnp.concatenate([so, sn], axis=3)
    e = jnp.exp(scores - jnp.max(scores, axis=3, keepdims=True))
    total = jnp.sum(e, axis=3)
    p = e.astype(jnp.bfloat16)
    w = jnp.einsum("rhtc,rchd->rthd", p[..., :cached], vo, preferred_element_type=jnp.float32)
    w = w + jnp.einsum("rhts,srhd->rthd", p[..., cached:], vn, preferred_element_type=jnp.float32)
    w = w / jnp.transpose(total, (0, 2, 1))[..., None]
    return w.astype(jnp.bfloat16).reshape(rows, steps, width)


def on_device(
    hidden_in,
    queries,
    new_keys,
    new_values,
    cache_keys,
    cache_values,
    cache_lengths,
    expert_ids,
    router_logits,
    norm_gain,
    out_sectioned,
    expert_sectioned,
    bucket_owner,
):
    steps, own_rows, width = hidden_in.shape
    rows = queries.shape[1]
    n_ep = lax.axis_size("ep")
    n_rep = lax.axis_size("rep")
    block = width // n_rep
    mine = own_rows * steps
    me = lax.axis_index("rep")
    owners = lax.all_to_all(
        jnp.broadcast_to(bucket_owner, (n_ep, n_rep)), "ep", 0, 0, tiled=True
    )
    bucket = jnp.argmax(owners == me, axis=1).astype(jnp.int32)
    heads = attention(queries, cache_keys, cache_values, new_keys, new_values, cache_lengths)
    partial = jnp.dot(
        heads.reshape(rows * steps, -1), out_sectioned, preferred_element_type=jnp.float32
    ).astype(jnp.bfloat16)
    parts = lax.all_to_all(partial.reshape(n_ep, mine, block), "ep", 0, 0, tiled=True)
    attended = jnp.sum(parts.astype(jnp.float32), axis=0).astype(jnp.bfloat16)
    attended = lax.all_to_all(
        jnp.broadcast_to(attended, (n_rep, mine, block)), "rep", 0, 0, tiled=True
    )
    own = jnp.transpose(hidden_in, (1, 0, 2)).reshape(mine, n_rep, block)
    residual = jnp.transpose(own, (1, 0, 2)).astype(jnp.float32) + attended.astype(jnp.float32)
    mean_square = jnp.sum(residual * residual, axis=(0, 2), keepdims=True) / width
    gain = norm_gain.reshape(n_rep, 1, block)
    normalized = (residual * lax.rsqrt(mean_square + EPSILON) * gain).astype(jnp.bfloat16)
    arrivals = lax.all_to_all(jnp.take(normalized, bucket, axis=0), "ep", 0, 0, tiled=True)
    arrivals = arrivals.reshape(n_ep * mine, block)
    weight = expert_sectioned[0]
    gate = jnp.dot(arrivals, weight[:, 0], preferred_element_type=jnp.float32)
    up = jnp.dot(arrivals, weight[:, 1], preferred_element_type=jnp.float32)
    both = jnp.concatenate([gate.astype(jnp.bfloat16), up.astype(jnp.bfloat16)], axis=1)
    hidden = gate.shape[1]
    both = lax.all_to_all(both.reshape(n_rep, -1, 2 * hidden), "rep", 0, 0, tiled=True)
    both = jnp.sum(both.astype(jnp.float32), axis=0)
    activated = (jax.nn.silu(both[:, :hidden]) * both[:, hidden:]).astype(jnp.bfloat16)
    activated = lax.all_to_all(
        jnp.broadcast_to(activated, (n_rep,) + activated.shape), "rep", 0, 0, tiled=True
    ).reshape(-1, hidden)
    out = jnp.einsum("nf,df->nd", activated, weight[:, 2], preferred_element_type=jnp.float32)
    out = out.astype(jnp.bfloat16).reshape(n_ep, mine, block)
    back = lax.all_to_all(out, "ep", 0, 0, tiled=True)
    affinity = jax.nn.sigmoid(router_logits)
    share = ROUTE_SCALE * affinity / jnp.sum(affinity, axis=2, keepdims=True)
    chosen = expert_ids[..., None] == jnp.arange(n_ep, dtype=jnp.int32)
    share = jnp.sum(jnp.where(chosen, share[..., None], 0.0), axis=2)
    share = jnp.transpose(share, (2, 1, 0)).reshape(n_ep, mine, 1)
    scaled = back.astype(jnp.float32) * share
    place = (bucket[None, :] == jnp.arange(n_rep, dtype=jnp.int32)[:, None]).astype(jnp.float32)
    routed = jnp.dot(
        place, scaled.reshape(n_ep, -1), precision=lax.Precision.HIGHEST
    ).astype(jnp.bfloat16)
    routed = lax.all_to_all(
        jnp.broadcast_to(routed, (n_rep,) + routed.shape), "rep", 0, 0, tiled=True
    )
    routed = jnp.sum(routed.astype(jnp.float32), axis=0).reshape(n_rep, mine, block)
    out = jnp.transpose((residual + routed).astype(jnp.bfloat16), (1, 0, 2))
    return jnp.transpose(out.reshape(own_rows, steps, width), (1, 0, 2))


def solution(mesh):
    return jax.shard_map(
        on_device,
        mesh=mesh,
        in_specs=(
            P(None, "ep", None),
            P(None, None, "ep"),
            P(None, None, "ep"),
            P(None, None, "ep"),
            P(None, None, "ep"),
            P(None, None, "ep"),
            P(),
            P(None, "ep", None),
            P(None, "ep", None),
            P(),
            P("ep", "rep"),
            P("ep", "rep", None, None),
            P("ep", None),
        ),
        out_specs=P(None, "ep", None),
        check_vma=False,
    )
```

```python
import math

import jax
import jax.numpy as jnp
from jax import lax
from jax.experimental import pallas as pl
from jax.experimental.pallas import tpu as pltpu
from jax.sharding import PartitionSpec as P

DH = 128
ROUTE_SCALE = 2.827
EPSILON = 1e-06
GROUP = 16
NEVER = -1e30
VMEM = pltpu.VMEM
SMEM = pltpu.SMEM
F32 = jnp.float32
BF16 = jnp.bfloat16


def dot_nt(a, b):
    return lax.dot_general(a, b, (((1,), (1,)), ((), ())), preferred_element_type=F32)


def attention_kernel(
    info_ref, q_ref, kn_ref, vn_ref, ck_ref, cv_ref, len_ref, out_ref, keep_ref, send_ref, heads
):
    g = pl.program_id(0)
    steps, _, width = q_ref.shape
    cached = ck_ref.shape[1]
    m = steps * GROUP
    n = GROUP * cached
    factor = 1.0 / math.sqrt(DH)
    row = lax.broadcasted_iota(jnp.int32, (m, n), 0)
    col = lax.broadcasted_iota(jnp.int32, (m, n), 1)
    lengths = jnp.concatenate([len_ref[...]] * steps, axis=0)
    live = (col // cached == row % GROUP) & (col % cached < lengths)
    row = lax.broadcasted_iota(jnp.int32, (m, m), 0)
    col = lax.broadcasted_iota(jnp.int32, (m, m), 1)
    recent = (col % GROUP == row % GROUP) & (col // GROUP <= row // GROUP)
    for h in range(width // DH):
        cut = slice(h * DH, (h + 1) * DH)
        q = q_ref[:, :, cut].reshape(m, DH)
        so = dot_nt(q, ck_ref[:, :, cut].reshape(n, DH)) * factor
        sn = dot_nt(q, kn_ref[:, :, cut].reshape(m, DH)) * factor
        so = jnp.where(live, so, NEVER)
        sn = jnp.where(recent, sn, NEVER)
        top = jnp.maximum(
            jnp.max(so, axis=1, keepdims=True), jnp.max(sn, axis=1, keepdims=True)
        )
        eo = jnp.exp(so - top)
        en = jnp.exp(sn - top)
        total = jnp.sum(eo, axis=1, keepdims=True) + jnp.sum(en, axis=1, keepdims=True)
        w = jnp.dot(
            eo.astype(BF16), cv_ref[:, :, cut].reshape(n, DH), preferred_element_type=F32
        ) + jnp.dot(
            en.astype(BF16), vn_ref[:, :, cut].reshape(m, DH), preferred_element_type=F32
        )
        heads[:, pl.ds(g * GROUP, GROUP), cut] = (w / total).astype(BF16).reshape(steps, GROUP, DH)

    @pl.when(g == pl.num_programs(0) - 1)
    def _():
        rows = heads.shape[1]
        every = steps * rows
        half = every // 2
        mine = keep_ref.shape[1]
        own = mine // steps
        parity = info_ref[0]
        j = lax.broadcasted_iota(jnp.int32, (every, every), 0)
        source = lax.broadcasted_iota(jnp.int32, (every, every), 1)
        side = j // half
        chip = (j % half) // mine
        step = (j % mine) // own
        core = jnp.where(side == 0, parity, 1 - parity)
        wanted = step * rows + (chip * 2 + core) * own + j % own
        order = jnp.where(source == wanted, 1.0, 0.0).astype(BF16)
        h = jnp.dot(order, heads[...].reshape(every, width), preferred_element_type=F32)
        part = jnp.dot(h.astype(BF16), out_ref[...], preferred_element_type=F32).astype(BF16)
        block = out_ref.shape[1]
        chips = half // mine
        keep_ref[:, :, :block] = part[:half].reshape(chips, mine, block)
        send_ref[:, :, :block] = part[half:].reshape(chips, mine, block)
        extra = keep_ref.shape[2] - block
        lane = lax.broadcasted_iota(jnp.int32, (chips, mine, extra), 2)
        bucket = info_ref[1]
        keep_ref[:, :, block:] = jnp.where(lane == 0, bucket, 0).astype(F32).astype(BF16)
        send_ref[:, :, block:] = jnp.where(lane == 1, bucket, 0).astype(F32).astype(BF16)


def attention(info, queries, new_keys, new_values, cache_keys, cache_values, lengths, out, chips):
    steps, rows, width = queries.shape
    cached = cache_keys.shape[1]
    block = out.shape[1]
    mine = steps * rows // (2 * chips)
    fresh = pl.BlockSpec((steps, GROUP, width), lambda g: (0, g, 0))
    old = pl.BlockSpec((GROUP, cached, width), lambda g: (g, 0, 0))
    shape = (chips, mine, block + 128)
    whole = pl.BlockSpec(shape, lambda g: (0, 0, 0))
    return pl.pallas_call(
        attention_kernel,
        grid=(rows // GROUP,),
        in_specs=[
            pl.BlockSpec(memory_space=SMEM),
            fresh,
            fresh,
            fresh,
            old,
            old,
            pl.BlockSpec((GROUP, 1), lambda g: (g, 0)),
            pl.BlockSpec(out.shape, lambda g: (0, 0)),
        ],
        out_specs=[whole, whole],
        out_shape=[jax.ShapeDtypeStruct(shape, BF16)] * 2,
        scratch_shapes=[VMEM((steps, rows, width), BF16)],
        name="attention",
    )(info, queries, new_keys, new_values, cache_keys, cache_values, lengths, out)


def select_kernel(bucket_ref, att_ref, hid_ref, gain_ref, out_ref, res, norm):
    blocks, rows, block = att_ref.shape
    total = jnp.zeros((rows, block), F32)
    for b in range(blocks):
        x = att_ref[b].astype(F32) + hid_ref[:, b * block : (b + 1) * block].astype(F32)
        res[b] = x
        total = total + x * x
    mean = jnp.sum(total, axis=1, keepdims=True) / (blocks * block)
    scale = lax.rsqrt(mean + EPSILON)
    for b in range(blocks):
        gain = gain_ref[:, b * block : (b + 1) * block]
        norm[b] = (res[b] * scale * gain).astype(BF16)
    for c in range(out_ref.shape[0]):
        out_ref[c] = norm[bucket_ref[c]]


def select(buckets, att, hid, gain):
    blocks, rows, block = att.shape
    chips = buckets.shape[0]
    vm = pl.BlockSpec(memory_space=VMEM)
    return pl.pallas_call(
        select_kernel,
        in_specs=[pl.BlockSpec(memory_space=SMEM), vm, vm, vm],
        out_specs=vm,
        out_shape=jax.ShapeDtypeStruct((chips, rows, block), BF16),
        scratch_shapes=[VMEM(att.shape, F32), VMEM(att.shape, BF16)],
        name="select",
    )(buckets, att, hid, gain)


def gate_up_kernel(x_ref, w_ref, out_ref):
    out_ref[...] = jnp.dot(x_ref[...], w_ref[0], preferred_element_type=F32).astype(BF16)


def gate_up(x, weight, tile=512):
    rows, block = x.shape
    hidden = weight.shape[2]
    per = hidden // tile
    return pl.pallas_call(
        gate_up_kernel,
        grid=(2 * per,),
        in_specs=[
            pl.BlockSpec((rows, block), lambda j: (0, 0)),
            pl.BlockSpec((1, block, tile), lambda j: (j // per, 0, j % per)),
        ],
        out_specs=pl.BlockSpec((rows, tile), lambda j: (0, j)),
        out_shape=jax.ShapeDtypeStruct((rows, 2 * hidden), BF16),
        name="gate_up",
    )(x, weight)


def down_kernel(x_ref, w_ref, out_ref):
    out_ref[...] = dot_nt(x_ref[...], w_ref[0]).astype(BF16)


def down(x, weight):
    rows, hidden = x.shape
    block = weight.shape[1]
    return pl.pallas_call(
        down_kernel,
        grid=(1,),
        in_specs=[
            pl.BlockSpec((rows, hidden), lambda j: (0, 0)),
            pl.BlockSpec((1, block, hidden), lambda j: (2, 0, 0)),
        ],
        out_specs=pl.BlockSpec((rows, block), lambda j: (0, 0)),
        out_shape=jax.ShapeDtypeStruct((rows, block), BF16),
        name="down",
    )(x, weight)


def combine_kernel(bucket_ref, share_ref, keep_ref, got_ref, out_ref, acc):
    acc[...] = jnp.zeros_like(acc)
    chips = keep_ref.shape[0]
    share = share_ref[...]
    for side, ref in enumerate((keep_ref, got_ref)):
        for c in range(chips):
            e = side * chips + c
            b = bucket_ref[e]
            acc[b] = acc[b] + share[:, e : e + 1] * ref[c].astype(F32)
    done = acc[...].astype(BF16)
    for r in range(out_ref.shape[0]):
        out_ref[r] = done


def combine(buckets, share, keep, got, ranks):
    _, rows, block = keep.shape
    vm = pl.BlockSpec(memory_space=VMEM)
    return pl.pallas_call(
        combine_kernel,
        in_specs=[pl.BlockSpec(memory_space=SMEM), vm, vm, vm],
        out_specs=vm,
        out_shape=jax.ShapeDtypeStruct((ranks, ranks, rows, block), BF16),
        scratch_shapes=[VMEM((ranks, rows, block), F32)],
        name="combine",
    )(buckets, share, keep, got)


def on_device(
    hidden_in,
    queries,
    new_keys,
    new_values,
    cache_keys,
    cache_values,
    cache_lengths,
    expert_ids,
    router_logits,
    norm_gain,
    out_sectioned,
    expert_sectioned,
    bucket_owner,
):
    steps, own_rows, width = hidden_in.shape
    n_ep = lax.axis_size("ep")
    n_rep = lax.axis_size("rep")
    chips = n_ep // 2
    block = width // n_rep
    mine = own_rows * steps
    rank = lax.axis_index("rep")
    parity = lax.axis_index("ep") % 2
    pair = [(j, j ^ 1) for j in range(n_ep)]
    cores = [[j for j in range(n_ep) if j % 2 == k] for k in range(2)]

    def swap(x):
        return lax.ppermute(x, "ep", pair)

    def across(x):
        return lax.all_to_all(x, "ep", 0, 0, tiled=True, axis_index_groups=cores)

    def over_rep(x):
        return lax.all_to_all(x, "rep", 0, 0, tiled=True)

    bucket = jnp.argmax(bucket_owner[0] == rank).astype(jnp.int32)
    info = jnp.stack([parity, bucket])
    own_hidden = hidden_in.reshape(mine, width)
    keep, send = attention(
        info,
        queries,
        new_keys,
        new_values,
        cache_keys,
        cache_values,
        cache_lengths[:, None],
        out_sectioned,
        chips,
    )
    both = (keep.astype(F32) + swap(send).astype(F32)).astype(BF16)
    parts = across(both)
    buckets = parts[:, 0, block : block + 2].astype(jnp.int32).T
    attended = jnp.sum(parts[:, :, :block].astype(F32), axis=0).astype(BF16)
    attended = jnp.concatenate([attended, swap(attended)], axis=0)
    attended = over_rep(jnp.broadcast_to(attended, (n_rep,) + attended.shape))
    hidden16 = jnp.concatenate([own_hidden, swap(own_hidden)], axis=0)
    chosen = select(buckets[0], attended, hidden16, norm_gain.reshape(1, width))
    arrivals = across(chosen).reshape(-1, block)
    weight = jnp.transpose(expert_sectioned[0], (1, 0, 2))
    hidden = weight.shape[2]
    partial = gate_up(arrivals, weight)
    partial = over_rep(partial.reshape(n_rep, -1, 2 * hidden))
    partial = jnp.sum(partial.astype(F32), axis=0)
    activated = (jax.nn.silu(partial[:, :hidden]) * partial[:, hidden:]).astype(BF16)
    activated = over_rep(jnp.broadcast_to(activated, (n_rep,) + activated.shape))
    result = down(activated.reshape(-1, hidden), weight)
    back = across(result.reshape(chips, 2 * mine, block))
    affinity = jax.nn.sigmoid(router_logits)
    share = ROUTE_SCALE * affinity / jnp.sum(affinity, axis=2, keepdims=True)
    picked = expert_ids[..., None] == jnp.arange(n_ep, dtype=jnp.int32)
    share = jnp.sum(jnp.where(picked, share[..., None], 0.0), axis=2).reshape(mine, chips, 2)
    share = jnp.where(parity == 0, share, share[:, :, ::-1])
    share = jnp.transpose(share, (0, 2, 1)).reshape(mine, n_ep)
    routed = combine(buckets.reshape(-1), share, back[:, :mine], swap(back[:, mine:]), n_rep)
    routed = over_rep(routed)
    routed = jnp.sum(routed.astype(F32), axis=0)
    residual = jnp.transpose(own_hidden.reshape(mine, n_rep, block), (1, 0, 2)).astype(F32)
    residual = residual + attended[:, :mine].astype(F32)
    out = jnp.transpose((residual + routed).astype(BF16), (1, 0, 2))
    return out.reshape(steps, own_rows, width)


def solution(mesh):
    return jax.shard_map(
        on_device,
        mesh=mesh,
        in_specs=(
            P(None, "ep", None),
            P(None, None, "ep"),
            P(None, None, "ep"),
            P(None, None, "ep"),
            P(None, None, "ep"),
            P(None, None, "ep"),
            P(),
            P(None, "ep", None),
            P(None, "ep", None),
            P(),
            P("ep", "rep"),
            P("ep", "rep", None, None),
            P("ep", None),
        ),
        out_specs=P(None, "ep", None),
        check_vma=False,
    )
```

```python
import math

import jax
import jax.numpy as jnp
from jax import lax
from jax.experimental import pallas as pl
from jax.experimental.pallas import tpu as pltpu
from jax.sharding import PartitionSpec as P

DH = 128
ROUTE_SCALE = 2.827
EPSILON = 1e-06
GROUP = 16
NEVER = -1e30
VMEM = pltpu.VMEM
SMEM = pltpu.SMEM
F32 = jnp.float32
BF16 = jnp.bfloat16
MIB = 1024 * 1024
ROOM = pltpu.CompilerParams(vmem_limit_bytes=16 * MIB)
MOST = pltpu.CompilerParams(vmem_limit_bytes=49 * MIB)
FETCH = pltpu.CompilerParams(vmem_limit_bytes=58 * MIB)


def dot_nt(a, b):
    return lax.dot_general(a, b, (((1,), (1,)), ((), ())), preferred_element_type=F32)


def attention_kernel(
    owner_ref,
    len_ref,
    q_hbm,
    kn_hbm,
    vn_hbm,
    ck_hbm,
    cv_hbm,
    out_hbm,
    keep_ref,
    send_ref,
    q_ref,
    kn_ref,
    vn_ref,
    ck_ref,
    cv_ref,
    out_ref,
    heads,
    sems,
):
    steps, rows, width = q_hbm.shape
    cached = ck_hbm.shape[1]
    groups = rows // GROUP
    fresh = [
        pltpu.make_async_copy(src, dst, sems.at[i])
        for i, (src, dst) in enumerate(
            ((q_hbm, q_ref), (kn_hbm, kn_ref), (vn_hbm, vn_ref), (out_hbm, out_ref))
        )
    ]
    old = []
    for g in range(2):
        part = pl.ds(g * (rows // 2), rows // 2)
        for i, (src, dst) in enumerate(((ck_hbm, ck_ref), (cv_hbm, cv_ref))):
            sem = sems.at[4 + 2 * g + i]
            old.append(pltpu.make_async_copy(src.at[part], dst.at[part], sem))
    for copy in fresh[:3] + old + fresh[3:]:
        copy.start()
    rank = lax.axis_index("rep")
    parity = lax.axis_index("ep") % 2
    bucket = jnp.int32(0)
    for b in range(owner_ref.shape[1]):
        bucket = jnp.where(owner_ref[0, b] == rank, b, bucket)
    m = steps * GROUP
    n = GROUP * cached
    factor = 1.0 / math.sqrt(DH)
    row = lax.broadcasted_iota(jnp.int32, (m, n), 0)
    col = lax.broadcasted_iota(jnp.int32, (m, n), 1)
    own = col // cached == row % GROUP
    place = col % cached
    row = lax.broadcasted_iota(jnp.int32, (m, m), 0)
    col = lax.broadcasted_iota(jnp.int32, (m, m), 1)
    recent = (col % GROUP == row % GROUP) & (col // GROUP <= row // GROUP)
    row = lax.broadcasted_iota(jnp.int32, (m, rows), 0)
    col = lax.broadcasted_iota(jnp.int32, (m, rows), 1)
    lengths = len_ref[...].astype(F32)
    for copy in fresh[:3]:
        copy.wait()
    def score(g, h, live):
        part = slice(g * GROUP, (g + 1) * GROUP)
        cut = slice(h * DH, (h + 1) * DH)
        q = q_ref[:, part, cut].reshape(m, DH)
        so = dot_nt(q, ck_ref[part, :, cut].reshape(n, DH)) * factor
        sn = dot_nt(q, kn_ref[:, part, cut].reshape(m, DH)) * factor
        return jnp.where(live, so, NEVER), jnp.where(recent, sn, NEVER)

    def soften(so, sn):
        top = jnp.maximum(jnp.max(so, axis=1, keepdims=True), jnp.max(sn, axis=1, keepdims=True))
        eo = jnp.exp(so - top)
        en = jnp.exp(sn - top)
        total = jnp.sum(eo, axis=1, keepdims=True) + jnp.sum(en, axis=1, keepdims=True)
        return eo.astype(BF16), en.astype(BF16), 1.0 / total

    def gather(g, h, eo, en, inverse):
        part = slice(g * GROUP, (g + 1) * GROUP)
        cut = slice(h * DH, (h + 1) * DH)
        w = jnp.dot(
            eo, cv_ref[part, :, cut].reshape(n, DH), preferred_element_type=F32
        ) + jnp.dot(en, vn_ref[:, part, cut].reshape(m, DH), preferred_element_type=F32)
        return (w * inverse).astype(BF16).reshape(steps, GROUP, DH)

    scores = []
    for g in range(groups):
        if g % (groups // 2) == 0:
            for copy in old[g : g + 2]:
                copy.wait()
        length = jnp.sum(
            jnp.where(col == row % GROUP + g * GROUP, lengths, 0.0), axis=1, keepdims=True
        )
        live = own & (place < length.astype(jnp.int32))
        scores += [(g, h, *score(g, h, live)) for h in range(width // DH)]
    soft = [(g, h, *soften(so, sn)) for g, h, so, sn in scores]
    for g, h, *rest in soft:
        part = slice(g * GROUP, (g + 1) * GROUP)
        heads[:, part, h * DH : (h + 1) * DH] = gather(g, h, *rest)
    every = steps * rows
    half = every // 2
    mine = keep_ref.shape[1]
    own_rows = mine // steps
    j = lax.broadcasted_iota(jnp.int32, (every, 1), 0)
    core = jnp.where(j < half, parity, 1 - parity)
    chip = (j % half) // mine
    step = (j % mine) // own_rows
    wanted = step * rows + (chip * 2 + core) * own_rows + j % own_rows
    source = lax.broadcasted_iota(jnp.int32, (every, every), 1)
    order = jnp.where(source == wanted, 1.0, 0.0).astype(BF16)
    h = jnp.dot(order, heads[...].reshape(every, width), preferred_element_type=F32)
    h = h.astype(BF16)
    fresh[3].wait()
    block = out_ref.shape[1]
    chips = half // mine
    for side, ref in enumerate((keep_ref, send_ref)):
        part = jnp.dot(
            h[side * half : (side + 1) * half], out_ref[...], preferred_element_type=F32
        )
        ref[:, :, :block] = part.astype(BF16).reshape(chips, mine, block)
        lane = lax.broadcasted_iota(jnp.int32, (chips, mine, ref.shape[2] - block), 2)
        ref[:, :, block:] = jnp.where(lane == side, bucket, 0).astype(F32).astype(BF16)


def attention(owner, queries, new_keys, new_values, cache_keys, cache_values, lengths, out, chips):
    steps, rows, width = queries.shape
    mine = steps * rows // (2 * chips)
    shape = (chips, mine, out.shape[1] + 128)
    vm = pl.BlockSpec(memory_space=VMEM)
    hbm = pl.BlockSpec(memory_space=pltpu.HBM)
    operands = (queries, new_keys, new_values, cache_keys, cache_values, out)
    return pl.pallas_call(
        attention_kernel,
        in_specs=[pl.BlockSpec(memory_space=SMEM), vm] + [hbm] * len(operands),
        out_specs=[vm, vm],
        out_shape=[jax.ShapeDtypeStruct(shape, BF16)] * 2,
        scratch_shapes=[VMEM(x.shape, BF16) for x in operands]
        + [
            VMEM((steps, rows, width), BF16),
            pltpu.SemaphoreType.DMA((8,)),
        ],
        compiler_params=FETCH,
        name="attention",
    )(owner, lengths, *operands)


def select_kernel(bucket_ref, res_ref, gain_ref, out_ref, norm):
    blocks, rows, block = res_ref.shape
    total = jnp.zeros((rows, block), F32)
    for b in range(blocks):
        x = res_ref[b].astype(F32)
        total = total + x * x
    mean = jnp.sum(total, axis=1, keepdims=True) / (blocks * block)
    scale = lax.rsqrt(mean + EPSILON)
    for b in range(blocks):
        gain = gain_ref[:, b * block : (b + 1) * block]
        norm[b] = (res_ref[b].astype(F32) * scale * gain).astype(BF16)
    for c in range(out_ref.shape[0]):
        out_ref[c] = norm[bucket_ref[c]]


def select(buckets, residual, gain):
    blocks, rows, block = residual.shape
    chips = buckets.shape[0]
    vm = pl.BlockSpec(memory_space=VMEM)
    return pl.pallas_call(
        select_kernel,
        in_specs=[pl.BlockSpec(memory_space=SMEM), vm, vm],
        out_specs=vm,
        out_shape=jax.ShapeDtypeStruct((chips, rows, block), BF16),
        scratch_shapes=[VMEM(residual.shape, BF16)],
        compiler_params=ROOM,
        name="select",
    )(buckets, residual, gain)


def gate_up_kernel(x_ref, w_hbm, out_ref, w_ref, sems):
    hidden = w_ref.shape[2]
    tile = 256
    copies = [pltpu.make_async_copy(w_hbm.at[i], w_ref.at[i], sems.at[i]) for i in range(2)]
    for copy in copies:
        copy.start()
    for i, copy in enumerate(copies):
        copy.wait()
        for j in range(0, hidden, tile):
            part = jnp.dot(x_ref[...], w_ref[i, :, j : j + tile], preferred_element_type=F32)
            out_ref[:, i * hidden + j : i * hidden + j + tile] = part.astype(BF16)


def gate_up(x, weight):
    vm = pl.BlockSpec(memory_space=VMEM)
    hidden = weight.shape[2]
    return pl.pallas_call(
        gate_up_kernel,
        in_specs=[vm, pl.BlockSpec(memory_space=pltpu.HBM)],
        out_specs=vm,
        out_shape=jax.ShapeDtypeStruct((x.shape[0], 2 * hidden), BF16),
        scratch_shapes=[
            VMEM((2,) + weight.shape[1:], BF16),
            pltpu.SemaphoreType.DMA((2,)),
        ],
        compiler_params=MOST,
        name="gate_up",
    )(x, weight)


def down_kernel(x_ref, w_ref, out_ref):
    tile = 128
    for j in range(0, w_ref.shape[1], tile):
        out_ref[:, j : j + tile] = dot_nt(x_ref[...], w_ref[2, j : j + tile]).astype(BF16)


def down(x, weight):
    vm = pl.BlockSpec(memory_space=VMEM)
    return pl.pallas_call(
        down_kernel,
        in_specs=[vm, vm],
        out_specs=vm,
        out_shape=jax.ShapeDtypeStruct((x.shape[0], weight.shape[1]), BF16),
        compiler_params=ROOM,
        name="down",
    )(x, weight)


def combine_kernel(bucket_ref, ids_ref, logits_ref, keep_ref, got_ref, out_ref, acc):
    chips, rows, block = keep_ref.shape
    steps = ids_ref.shape[0]
    ids = jnp.concatenate([ids_ref[t] for t in range(steps)], axis=0)
    logits = jnp.concatenate([logits_ref[t] for t in range(steps)], axis=0)
    affinity = 1.0 / (1.0 + jnp.exp(-logits))
    weight = ROUTE_SCALE * affinity / jnp.sum(affinity, axis=1, keepdims=True)
    parity = lax.axis_index("ep") % 2
    col = lax.broadcasted_iota(jnp.int32, (rows, 2 * chips), 1)
    expert = jnp.where(col < chips, 2 * col + parity, 2 * (col - chips) + 1 - parity)
    share = jnp.zeros((rows, 2 * chips), F32)
    for k in range(ids.shape[1]):
        share = share + jnp.where(ids[:, k : k + 1] == expert, weight[:, k : k + 1], 0.0)
    acc[...] = jnp.zeros_like(acc)
    for side, ref in enumerate((keep_ref, got_ref)):
        for c in range(chips):
            e = side * chips + c
            b = bucket_ref[e]
            acc[b] = acc[b] + share[:, e : e + 1] * ref[c].astype(F32)
    done = acc[...].astype(BF16)
    for r in range(out_ref.shape[0]):
        out_ref[r] = done


def combine(buckets, ids, logits, keep, got, ranks):
    _, rows, block = keep.shape
    vm = pl.BlockSpec(memory_space=VMEM)
    return pl.pallas_call(
        combine_kernel,
        in_specs=[pl.BlockSpec(memory_space=SMEM), vm, vm, vm, vm],
        out_specs=vm,
        out_shape=jax.ShapeDtypeStruct((ranks, ranks, rows, block), BF16),
        scratch_shapes=[VMEM((ranks, rows, block), F32)],
        compiler_params=ROOM,
        name="combine",
    )(buckets, ids, logits, keep, got)


def finish_kernel(part_ref, res_ref, out_ref):
    ranks, blocks, rows, block = part_ref.shape
    own = out_ref.shape[1]
    for b in range(blocks):
        x = res_ref[b, :rows].astype(F32)
        for r in range(ranks):
            x = x + part_ref[r, b].astype(F32)
        for t in range(out_ref.shape[0]):
            row = x[t * own : (t + 1) * own].astype(BF16)
            out_ref[t, :, b * block : (b + 1) * block] = row


def finish(parts, residual, steps, own):
    _, blocks, _, block = parts.shape
    vm = pl.BlockSpec(memory_space=VMEM)
    return pl.pallas_call(
        finish_kernel,
        in_specs=[vm, vm],
        out_specs=vm,
        out_shape=jax.ShapeDtypeStruct((steps, own, blocks * block), BF16),
        compiler_params=ROOM,
        name="finish",
    )(parts, residual)


def on_device(
    hidden_in,
    queries,
    new_keys,
    new_values,
    cache_keys,
    cache_values,
    cache_lengths,
    expert_ids,
    router_logits,
    norm_gain,
    out_sectioned,
    expert_sectioned,
    bucket_owner,
):
    steps, own_rows, width = hidden_in.shape
    n_ep = lax.axis_size("ep")
    n_rep = lax.axis_size("rep")
    chips = n_ep // 2
    block = width // n_rep
    mine = own_rows * steps
    rank = lax.axis_index("rep")
    pair = [(j, j ^ 1) for j in range(n_ep)]
    cores = [[j for j in range(n_ep) if j % 2 == k] for k in range(2)]

    def swap(x):
        return lax.ppermute(x, "ep", pair)

    def across(x):
        return lax.all_to_all(x, "ep", 0, 0, tiled=True, axis_index_groups=cores)

    def over_rep(x):
        return lax.all_to_all(x, "rep", 0, 0, tiled=True)

    keep, send = attention(
        bucket_owner,
        queries,
        new_keys,
        new_values,
        cache_keys,
        cache_values,
        cache_lengths[None],
        out_sectioned,
        chips,
    )
    parts = across((keep.astype(F32) + swap(send).astype(F32)).astype(BF16))
    buckets = parts[:, 0, block : block + 2].astype(jnp.int32).T
    own_buckets, buckets = buckets[0], buckets.reshape(-1)
    own_block = lax.dynamic_slice_in_dim(hidden_in, rank * block, block, 2).reshape(mine, block)
    residual = jnp.sum(parts[:, :, :block].astype(F32), axis=0) + own_block.astype(F32)
    residual = residual.astype(BF16)
    residual = jnp.concatenate([residual, swap(residual)], axis=0)
    residual = over_rep(jnp.broadcast_to(residual, (n_rep,) + residual.shape))
    residual, own_buckets, buckets = lax.optimization_barrier((residual, own_buckets, buckets))
    chosen = select(own_buckets, residual, norm_gain.reshape(1, width))
    arrivals = across(chosen).reshape(-1, block)
    weight = jnp.transpose(expert_sectioned[0], (1, 0, 2))
    hidden = weight.shape[2]
    partial = gate_up(arrivals, weight)
    partial = over_rep(partial.reshape(n_rep, -1, 2 * hidden))
    partial = jnp.sum(partial.astype(F32), axis=0)
    activated = (jax.nn.silu(partial[:, :hidden]) * partial[:, hidden:]).astype(BF16)
    activated = over_rep(jnp.broadcast_to(activated, (n_rep,) + activated.shape))
    result = down(activated.reshape(-1, hidden), weight)
    back = across(result.reshape(chips, 2 * mine, block))
    routed = combine(
        buckets, expert_ids, router_logits, back[:, :mine], swap(back[:, mine:]), n_rep
    )
    return finish(over_rep(routed), residual, steps, own_rows)


def solution(mesh):
    return jax.shard_map(
        on_device,
        mesh=mesh,
        in_specs=(
            P(None, "ep", None),
            P(None, None, "ep"),
            P(None, None, "ep"),
            P(None, None, "ep"),
            P(None, None, "ep"),
            P(None, None, "ep"),
            P(),
            P(None, "ep", None),
            P(None, "ep", None),
            P(),
            P("ep", "rep"),
            P("ep", "rep", None, None),
            P("ep", None),
        ),
        out_specs=P(None, "ep", None),
        check_vma=False,
    )
```

```python
import math

import jax
import jax.numpy as jnp
from jax import lax
from jax.experimental import pallas as pl
from jax.experimental.pallas import tpu as pltpu
from jax.sharding import PartitionSpec as P

DH = 128
ROUTE_SCALE = 2.827
EPSILON = 1e-06
GROUP = 16
NEVER = -1e30
VMEM = pltpu.VMEM
SMEM = pltpu.SMEM
F32 = jnp.float32
BF16 = jnp.bfloat16
MIB = 1024 * 1024
ROOM = pltpu.CompilerParams(vmem_limit_bytes=16 * MIB)
MOST = pltpu.CompilerParams(vmem_limit_bytes=49 * MIB)
FETCH = pltpu.CompilerParams(vmem_limit_bytes=58 * MIB)


def dot_nt(a, b):
    return lax.dot_general(a, b, (((1,), (1,)), ((), ())), preferred_element_type=F32)


def attention_kernel(
    owner_ref,
    len_ref,
    q_hbm,
    kn_hbm,
    vn_hbm,
    ck_hbm,
    cv_hbm,
    out_hbm,
    keep_ref,
    send_ref,
    q_ref,
    kn_ref,
    vn_ref,
    ck_ref,
    cv_ref,
    out_ref,
    heads,
    sems,
):
    steps, rows, width = q_hbm.shape
    cached = ck_hbm.shape[1]
    groups = rows // GROUP
    fresh = [
        pltpu.make_async_copy(src, dst, sems.at[i])
        for i, (src, dst) in enumerate(
            ((q_hbm, q_ref), (kn_hbm, kn_ref), (vn_hbm, vn_ref), (out_hbm, out_ref))
        )
    ]
    old = []
    for g in range(2):
        part = pl.ds(g * (rows // 2), rows // 2)
        for i, (src, dst) in enumerate(((ck_hbm, ck_ref), (cv_hbm, cv_ref))):
            sem = sems.at[4 + 2 * g + i]
            old.append(pltpu.make_async_copy(src.at[part], dst.at[part], sem))
    for copy in fresh[:3] + old + fresh[3:]:
        copy.start()
    rank = lax.axis_index("rep")
    parity = lax.axis_index("ep") % 2
    bucket = jnp.int32(0)
    for b in range(owner_ref.shape[1]):
        bucket = jnp.where(owner_ref[0, b] == rank, b, bucket)
    m = steps * GROUP
    n = GROUP * cached
    factor = 1.0 / math.sqrt(DH)
    row = lax.broadcasted_iota(jnp.int32, (m, n), 0)
    col = lax.broadcasted_iota(jnp.int32, (m, n), 1)
    own = col // cached == row % GROUP
    place = col % cached
    row = lax.broadcasted_iota(jnp.int32, (m, m), 0)
    col = lax.broadcasted_iota(jnp.int32, (m, m), 1)
    recent = (col % GROUP == row % GROUP) & (col // GROUP <= row // GROUP)
    row = lax.broadcasted_iota(jnp.int32, (m, rows), 0)
    col = lax.broadcasted_iota(jnp.int32, (m, rows), 1)
    lengths = len_ref[...].astype(F32)
    for copy in fresh[:3]:
        copy.wait()
    def score(g, h, live):
        part = slice(g * GROUP, (g + 1) * GROUP)
        cut = slice(h * DH, (h + 1) * DH)
        q = q_ref[:, part, cut].reshape(m, DH)
        so = dot_nt(q, ck_ref[part, :, cut].reshape(n, DH)) * factor
        sn = dot_nt(q, kn_ref[:, part, cut].reshape(m, DH)) * factor
        return jnp.where(live, so, NEVER), jnp.where(recent, sn, NEVER)

    def soften(so, sn):
        top = jnp.maximum(jnp.max(so, axis=1, keepdims=True), jnp.max(sn, axis=1, keepdims=True))
        eo = jnp.exp(so - top)
        en = jnp.exp(sn - top)
        total = jnp.sum(eo, axis=1, keepdims=True) + jnp.sum(en, axis=1, keepdims=True)
        return eo.astype(BF16), en.astype(BF16), 1.0 / total

    def gather(g, h, eo, en, inverse):
        part = slice(g * GROUP, (g + 1) * GROUP)
        cut = slice(h * DH, (h + 1) * DH)
        w = jnp.dot(
            eo, cv_ref[part, :, cut].reshape(n, DH), preferred_element_type=F32
        ) + jnp.dot(en, vn_ref[:, part, cut].reshape(m, DH), preferred_element_type=F32)
        return (w * inverse).astype(BF16).reshape(steps, GROUP, DH)

    scores = []
    for g in range(groups):
        if g % (groups // 2) == 0:
            for copy in old[g : g + 2]:
                copy.wait()
        length = jnp.sum(
            jnp.where(col == row % GROUP + g * GROUP, lengths, 0.0), axis=1, keepdims=True
        )
        live = own & (place < length.astype(jnp.int32))
        scores += [(g, h, *score(g, h, live)) for h in range(width // DH)]
    soft = [(g, h, *soften(so, sn)) for g, h, so, sn in scores]
    for g, h, *rest in soft:
        part = slice(g * GROUP, (g + 1) * GROUP)
        heads[:, part, h * DH : (h + 1) * DH] = gather(g, h, *rest)
    every = steps * rows
    half = every // 2
    mine = keep_ref.shape[1]
    own_rows = mine // steps
    j = lax.broadcasted_iota(jnp.int32, (every, 1), 0)
    core = jnp.where(j < half, parity, 1 - parity)
    chip = (j % half) // mine
    step = (j % mine) // own_rows
    wanted = step * rows + (chip * 2 + core) * own_rows + j % own_rows
    source = lax.broadcasted_iota(jnp.int32, (every, every), 1)
    order = jnp.where(source == wanted, 1.0, 0.0).astype(BF16)
    h = jnp.dot(order, heads[...].reshape(every, width), preferred_element_type=F32)
    h = h.astype(BF16)
    fresh[3].wait()
    block = out_ref.shape[1]
    chips = half // mine
    for side, ref in enumerate((keep_ref, send_ref)):
        part = jnp.dot(
            h[side * half : (side + 1) * half], out_ref[...], preferred_element_type=F32
        )
        ref[:, :, :block] = part.astype(BF16).reshape(chips, mine, block)
        lane = lax.broadcasted_iota(jnp.int32, (chips, mine, ref.shape[2] - block), 2)
        ref[:, :, block:] = jnp.where(lane == side, bucket, 0).astype(F32).astype(BF16)


def attention(owner, queries, new_keys, new_values, cache_keys, cache_values, lengths, out, chips):
    steps, rows, width = queries.shape
    mine = steps * rows // (2 * chips)
    shape = (chips, mine, out.shape[1] + 128)
    vm = pl.BlockSpec(memory_space=VMEM)
    hbm = pl.BlockSpec(memory_space=pltpu.HBM)
    operands = (queries, new_keys, new_values, cache_keys, cache_values, out)
    return pl.pallas_call(
        attention_kernel,
        in_specs=[pl.BlockSpec(memory_space=SMEM), vm] + [hbm] * len(operands),
        out_specs=[vm, vm],
        out_shape=[jax.ShapeDtypeStruct(shape, BF16)] * 2,
        scratch_shapes=[VMEM(x.shape, BF16) for x in operands]
        + [
            VMEM((steps, rows, width), BF16),
            pltpu.SemaphoreType.DMA((8,)),
        ],
        compiler_params=FETCH,
        name="attention",
    )(owner, lengths, *operands)


def select_kernel(bucket_ref, res_ref, gain_ref, out_ref, norm):
    blocks, rows, block = res_ref.shape
    total = jnp.zeros((rows, block), F32)
    for b in range(blocks):
        x = res_ref[b].astype(F32)
        total = total + x * x
    mean = jnp.sum(total, axis=1, keepdims=True) / (blocks * block)
    scale = lax.rsqrt(mean + EPSILON)
    for b in range(blocks):
        gain = gain_ref[:, b * block : (b + 1) * block]
        norm[b] = (res_ref[b].astype(F32) * scale * gain).astype(BF16)
    for c in range(out_ref.shape[0]):
        out_ref[c] = norm[bucket_ref[c]]


def select(buckets, residual, gain):
    blocks, rows, block = residual.shape
    chips = buckets.shape[0]
    vm = pl.BlockSpec(memory_space=VMEM)
    return pl.pallas_call(
        select_kernel,
        in_specs=[pl.BlockSpec(memory_space=SMEM), vm, vm],
        out_specs=vm,
        out_shape=jax.ShapeDtypeStruct((chips, rows, block), BF16),
        scratch_shapes=[VMEM(residual.shape, BF16)],
        compiler_params=ROOM,
        name="select",
    )(buckets, residual, gain)


def fetch_kernel(w_hbm, out_ref, sem):
    copy = pltpu.make_async_copy(w_hbm.at[pl.ds(0, out_ref.shape[0])], out_ref, sem)
    copy.start()
    copy.wait()


def fetch(weight, count):
    return pl.pallas_call(
        fetch_kernel,
        in_specs=[pl.BlockSpec(memory_space=pltpu.HBM)],
        out_specs=pl.BlockSpec(memory_space=VMEM),
        out_shape=jax.ShapeDtypeStruct((count,) + weight.shape[1:], BF16),
        scratch_shapes=[pltpu.SemaphoreType.DMA],
        compiler_params=MOST,
        name="fetch",
    )(weight)


def gate_up_kernel(x_ref, w_ref, out_ref):
    hidden = w_ref.shape[2]
    tile = 256
    for i in range(2):
        for j in range(0, hidden, tile):
            part = jnp.dot(x_ref[...], w_ref[i, :, j : j + tile], preferred_element_type=F32)
            out_ref[:, i * hidden + j : i * hidden + j + tile] = part.astype(BF16)


def gate_up(x, weight):
    vm = pl.BlockSpec(memory_space=VMEM)
    return pl.pallas_call(
        gate_up_kernel,
        in_specs=[vm, vm],
        out_specs=vm,
        out_shape=jax.ShapeDtypeStruct((x.shape[0], 2 * weight.shape[2]), BF16),
        compiler_params=ROOM,
        name="gate_up",
    )(x, weight)


def down_kernel(x_ref, w_ref, out_ref):
    tile = 128
    for j in range(0, w_ref.shape[1], tile):
        out_ref[:, j : j + tile] = dot_nt(x_ref[...], w_ref[2, j : j + tile]).astype(BF16)


def down(x, weight):
    vm = pl.BlockSpec(memory_space=VMEM)
    return pl.pallas_call(
        down_kernel,
        in_specs=[vm, vm],
        out_specs=vm,
        out_shape=jax.ShapeDtypeStruct((x.shape[0], weight.shape[1]), BF16),
        compiler_params=ROOM,
        name="down",
    )(x, weight)


def combine_kernel(bucket_ref, ids_ref, logits_ref, keep_ref, got_ref, out_ref, acc):
    chips, rows, block = keep_ref.shape
    steps = ids_ref.shape[0]
    ids = jnp.concatenate([ids_ref[t] for t in range(steps)], axis=0)
    logits = jnp.concatenate([logits_ref[t] for t in range(steps)], axis=0)
    affinity = 1.0 / (1.0 + jnp.exp(-logits))
    weight = ROUTE_SCALE * affinity / jnp.sum(affinity, axis=1, keepdims=True)
    parity = lax.axis_index("ep") % 2
    col = lax.broadcasted_iota(jnp.int32, (rows, 2 * chips), 1)
    expert = jnp.where(col < chips, 2 * col + parity, 2 * (col - chips) + 1 - parity)
    share = jnp.zeros((rows, 2 * chips), F32)
    for k in range(ids.shape[1]):
        share = share + jnp.where(ids[:, k : k + 1] == expert, weight[:, k : k + 1], 0.0)
    acc[...] = jnp.zeros_like(acc)
    for side, ref in enumerate((keep_ref, got_ref)):
        for c in range(chips):
            e = side * chips + c
            b = bucket_ref[e]
            acc[b] = acc[b] + share[:, e : e + 1] * ref[c].astype(F32)
    done = acc[...].astype(BF16)
    for r in range(out_ref.shape[0]):
        out_ref[r] = done


def combine(buckets, ids, logits, keep, got, ranks):
    _, rows, block = keep.shape
    vm = pl.BlockSpec(memory_space=VMEM)
    return pl.pallas_call(
        combine_kernel,
        in_specs=[pl.BlockSpec(memory_space=SMEM), vm, vm, vm, vm],
        out_specs=vm,
        out_shape=jax.ShapeDtypeStruct((ranks, ranks, rows, block), BF16),
        scratch_shapes=[VMEM((ranks, rows, block), F32)],
        compiler_params=ROOM,
        name="combine",
    )(buckets, ids, logits, keep, got)


def finish_kernel(part_ref, res_ref, out_ref):
    ranks, blocks, rows, block = part_ref.shape
    own = out_ref.shape[1]
    for b in range(blocks):
        x = res_ref[b, :rows].astype(F32)
        for r in range(ranks):
            x = x + part_ref[r, b].astype(F32)
        for t in range(out_ref.shape[0]):
            row = x[t * own : (t + 1) * own].astype(BF16)
            out_ref[t, :, b * block : (b + 1) * block] = row


def finish(parts, residual, steps, own):
    _, blocks, _, block = parts.shape
    vm = pl.BlockSpec(memory_space=VMEM)
    return pl.pallas_call(
        finish_kernel,
        in_specs=[vm, vm],
        out_specs=vm,
        out_shape=jax.ShapeDtypeStruct((steps, own, blocks * block), BF16),
        compiler_params=ROOM,
        name="finish",
    )(parts, residual)


def on_device(
    hidden_in,
    queries,
    new_keys,
    new_values,
    cache_keys,
    cache_values,
    cache_lengths,
    expert_ids,
    router_logits,
    norm_gain,
    out_sectioned,
    expert_sectioned,
    bucket_owner,
):
    steps, own_rows, width = hidden_in.shape
    n_ep = lax.axis_size("ep")
    n_rep = lax.axis_size("rep")
    chips = n_ep // 2
    block = width // n_rep
    mine = own_rows * steps
    rank = lax.axis_index("rep")
    pair = [(j, j ^ 1) for j in range(n_ep)]
    cores = [[j for j in range(n_ep) if j % 2 == k] for k in range(2)]

    def swap(x):
        return lax.ppermute(x, "ep", pair)

    def across(x):
        return lax.all_to_all(x, "ep", 0, 0, tiled=True, axis_index_groups=cores)

    def over_rep(x):
        return lax.all_to_all(x, "rep", 0, 0, tiled=True)

    keep, send = attention(
        bucket_owner,
        queries,
        new_keys,
        new_values,
        cache_keys,
        cache_values,
        cache_lengths[None],
        out_sectioned,
        chips,
    )
    own_block = lax.dynamic_slice_in_dim(hidden_in, rank * block, block, 2).reshape(mine, block)
    both = (keep.astype(F32) + swap(send).astype(F32)).astype(BF16)
    both, own_block = lax.optimization_barrier((both, own_block))
    parts = across(both)
    buckets = parts[:, 0, block : block + 2].astype(jnp.int32).T
    own_buckets, buckets = buckets[0], buckets.reshape(-1)
    residual = jnp.sum(parts[:, :, :block].astype(F32), axis=0) + own_block.astype(F32)
    residual = residual.astype(BF16)
    weight = jnp.transpose(expert_sectioned[0], (1, 0, 2))
    residual, weight = lax.optimization_barrier((residual, weight))
    other = swap(residual)
    into = fetch(weight, 2)
    other, into, own_buckets, buckets = lax.optimization_barrier(
        (other, into, own_buckets, buckets)
    )
    residual = jnp.concatenate([residual, other], axis=0)
    residual = over_rep(jnp.broadcast_to(residual, (n_rep,) + residual.shape))
    chosen = select(own_buckets, residual, norm_gain.reshape(1, width))
    arrivals = across(chosen).reshape(-1, block)
    hidden = weight.shape[2]
    partial = gate_up(arrivals, into)
    partial = over_rep(partial.reshape(n_rep, -1, 2 * hidden))
    partial = jnp.sum(partial.astype(F32), axis=0)
    activated = (jax.nn.silu(partial[:, :hidden]) * partial[:, hidden:]).astype(BF16)
    activated = over_rep(jnp.broadcast_to(activated, (n_rep,) + activated.shape))
    result = down(activated.reshape(-1, hidden), weight)
    back = across(result.reshape(chips, 2 * mine, block))
    routed = combine(
        buckets, expert_ids, router_logits, back[:, :mine], swap(back[:, mine:]), n_rep
    )
    return finish(over_rep(routed), residual, steps, own_rows)


def solution(mesh):
    return jax.shard_map(
        on_device,
        mesh=mesh,
        in_specs=(
            P(None, "ep", None),
            P(None, None, "ep"),
            P(None, None, "ep"),
            P(None, None, "ep"),
            P(None, None, "ep"),
            P(None, None, "ep"),
            P(),
            P(None, "ep", None),
            P(None, "ep", None),
            P(),
            P("ep", "rep"),
            P("ep", "rep", None, None),
            P("ep", None),
        ),
        out_specs=P(None, "ep", None),
        check_vma=False,
    )
```

```python
import math

import jax
import jax.numpy as jnp
from jax import lax
from jax.experimental import pallas as pl
from jax.experimental.pallas import tpu as pltpu
from jax.sharding import PartitionSpec as P

DH = 128
ROUTE_SCALE = 2.827
EPSILON = 1e-06
GROUP = 16
NEVER = -1e30
VMEM = pltpu.VMEM
SMEM = pltpu.SMEM
F32 = jnp.float32
BF16 = jnp.bfloat16
MIB = 1024 * 1024
ROOM = pltpu.CompilerParams(vmem_limit_bytes=16 * MIB)
MOST = pltpu.CompilerParams(vmem_limit_bytes=49 * MIB)
FETCH = pltpu.CompilerParams(vmem_limit_bytes=58 * MIB)


def dot_nt(a, b):
    return lax.dot_general(a, b, (((1,), (1,)), ((), ())), preferred_element_type=F32)


def attention_kernel(
    owner_hbm,
    len_hbm,
    q_hbm,
    kn_hbm,
    vn_hbm,
    ck_hbm,
    cv_hbm,
    out_hbm,
    keep_ref,
    send_ref,
    owner_ref,
    len_ref,
    q_ref,
    kn_ref,
    vn_ref,
    ck_ref,
    cv_ref,
    out_ref,
    heads,
    sems,
):
    steps, rows, width = q_hbm.shape
    cached = ck_hbm.shape[1]
    groups = rows // GROUP
    fresh = [
        pltpu.make_async_copy(src, dst, sems.at[i])
        for i, (src, dst) in enumerate(
            ((q_hbm, q_ref), (kn_hbm, kn_ref), (vn_hbm, vn_ref), (out_hbm, out_ref))
        )
    ]
    small = [
        pltpu.make_async_copy(len_hbm, len_ref, sems.at[8]),
        pltpu.make_async_copy(owner_hbm, owner_ref, sems.at[9]),
    ]
    old = []
    for g in range(2):
        part = pl.ds(g * (rows // 2), rows // 2)
        for i, (src, dst) in enumerate(((ck_hbm, ck_ref), (cv_hbm, cv_ref))):
            sem = sems.at[4 + 2 * g + i]
            old.append(pltpu.make_async_copy(src.at[part], dst.at[part], sem))
    for copy in fresh[:3] + old[:1] + small + old[1:] + fresh[3:]:
        copy.start()
    parity = lax.axis_index("ep") % 2
    m = steps * GROUP
    n = GROUP * cached
    factor = 1.0 / math.sqrt(DH)
    row = lax.broadcasted_iota(jnp.int32, (m, n), 0)
    col = lax.broadcasted_iota(jnp.int32, (m, n), 1)
    own = col // cached == row % GROUP
    place = col % cached
    row = lax.broadcasted_iota(jnp.int32, (m, m), 0)
    col = lax.broadcasted_iota(jnp.int32, (m, m), 1)
    recent = (col % GROUP == row % GROUP) & (col // GROUP <= row // GROUP)
    row = lax.broadcasted_iota(jnp.int32, (m, rows), 0)
    col = lax.broadcasted_iota(jnp.int32, (m, rows), 1)
    for copy in fresh[:3] + small[:1]:
        copy.wait()
    lengths = len_ref[...].astype(F32)
    def score(g, h, live):
        part = slice(g * GROUP, (g + 1) * GROUP)
        cut = slice(h * DH, (h + 1) * DH)
        q = q_ref[:, part, cut].reshape(m, DH)
        so = dot_nt(q, ck_ref[part, :, cut].reshape(n, DH)) * factor
        sn = dot_nt(q, kn_ref[:, part, cut].reshape(m, DH)) * factor
        return jnp.where(live, so, NEVER), jnp.where(recent, sn, NEVER)

    def soften(so, sn):
        top = jnp.maximum(jnp.max(so, axis=1, keepdims=True), jnp.max(sn, axis=1, keepdims=True))
        eo = jnp.exp(so - top)
        en = jnp.exp(sn - top)
        total = jnp.sum(eo, axis=1, keepdims=True) + jnp.sum(en, axis=1, keepdims=True)
        return eo.astype(BF16), en.astype(BF16), 1.0 / total

    def gather(g, h, eo, en, inverse):
        part = slice(g * GROUP, (g + 1) * GROUP)
        cut = slice(h * DH, (h + 1) * DH)
        w = jnp.dot(
            eo, cv_ref[part, :, cut].reshape(n, DH), preferred_element_type=F32
        ) + jnp.dot(en, vn_ref[:, part, cut].reshape(m, DH), preferred_element_type=F32)
        return (w * inverse).astype(BF16).reshape(steps, GROUP, DH)

    scores = []
    for g in range(groups):
        if g % (groups // 2) == 0:
            for copy in old[g : g + 2]:
                copy.wait()
        length = jnp.sum(
            jnp.where(col == row % GROUP + g * GROUP, lengths, 0.0), axis=1, keepdims=True
        )
        live = own & (place < length.astype(jnp.int32))
        scores += [(g, h, *score(g, h, live)) for h in range(width // DH)]
    soft = [(g, h, *soften(so, sn)) for g, h, so, sn in scores]
    for g, h, *rest in soft:
        part = slice(g * GROUP, (g + 1) * GROUP)
        heads[:, part, h * DH : (h + 1) * DH] = gather(g, h, *rest)
    every = steps * rows
    half = every // 2
    mine = keep_ref.shape[1]
    own_rows = mine // steps
    j = lax.broadcasted_iota(jnp.int32, (every, 1), 0)
    core = jnp.where(j < half, parity, 1 - parity)
    chip = (j % half) // mine
    step = (j % mine) // own_rows
    wanted = step * rows + (chip * 2 + core) * own_rows + j % own_rows
    source = lax.broadcasted_iota(jnp.int32, (every, every), 1)
    order = jnp.where(source == wanted, 1.0, 0.0).astype(BF16)
    h = jnp.dot(order, heads[...].reshape(every, width), preferred_element_type=F32)
    h = h.astype(BF16)
    small[1].wait()
    rank = lax.axis_index("rep")
    bucket = jnp.int32(0)
    for b in range(owner_ref.shape[1]):
        bucket = jnp.where(owner_ref[0, b] == rank, b, bucket)
    fresh[3].wait()
    block = out_ref.shape[1]
    chips = half // mine
    for side, ref in enumerate((keep_ref, send_ref)):
        part = jnp.dot(
            h[side * half : (side + 1) * half], out_ref[...], preferred_element_type=F32
        )
        ref[:, :, :block] = part.astype(BF16).reshape(chips, mine, block)
        lane = lax.broadcasted_iota(jnp.int32, (chips, mine, ref.shape[2] - block), 2)
        ref[:, :, block:] = jnp.where(lane == side, bucket, 0).astype(F32).astype(BF16)


def attention(owner, queries, new_keys, new_values, cache_keys, cache_values, lengths, out, chips):
    steps, rows, width = queries.shape
    mine = steps * rows // (2 * chips)
    shape = (chips, mine, out.shape[1] + 128)
    vm = pl.BlockSpec(memory_space=VMEM)
    hbm = pl.BlockSpec(memory_space=pltpu.HBM)
    operands = (queries, new_keys, new_values, cache_keys, cache_values, out)
    return pl.pallas_call(
        attention_kernel,
        in_specs=[hbm] * (2 + len(operands)),
        out_specs=[vm, vm],
        out_shape=[jax.ShapeDtypeStruct(shape, BF16)] * 2,
        scratch_shapes=[SMEM(owner.shape, jnp.int32), VMEM(lengths.shape, jnp.int32)]
        + [VMEM(x.shape, BF16) for x in operands]
        + [
            VMEM((steps, rows, width), BF16),
            pltpu.SemaphoreType.DMA((10,)),
        ],
        compiler_params=FETCH,
        name="attention",
    )(owner, lengths, *operands)


def select_kernel(bucket_any, res_ref, gain_ref, out_ref, norm, bucket_ref, sem):
    fetch_buckets = pltpu.make_async_copy(bucket_any, bucket_ref, sem)
    fetch_buckets.start()
    blocks, rows, block = res_ref.shape
    total = jnp.zeros((rows, block), F32)
    for b in range(blocks):
        x = res_ref[b].astype(F32)
        total = total + x * x
    mean = jnp.sum(total, axis=1, keepdims=True) / (blocks * block)
    scale = lax.rsqrt(mean + EPSILON)
    for b in range(blocks):
        gain = gain_ref[:, b * block : (b + 1) * block]
        norm[b] = (res_ref[b].astype(F32) * scale * gain).astype(BF16)
    fetch_buckets.wait()
    for c in range(out_ref.shape[0]):
        out_ref[c] = norm[bucket_ref[c]]


def select(buckets, residual, gain):
    blocks, rows, block = residual.shape
    chips = buckets.shape[0]
    vm = pl.BlockSpec(memory_space=VMEM)
    return pl.pallas_call(
        select_kernel,
        in_specs=[pl.BlockSpec(memory_space=pl.ANY), vm, vm],
        out_specs=vm,
        out_shape=jax.ShapeDtypeStruct((chips, rows, block), BF16),
        scratch_shapes=[
            VMEM(residual.shape, BF16),
            SMEM(buckets.shape, jnp.int32),
            pltpu.SemaphoreType.DMA,
        ],
        compiler_params=ROOM,
        name="select",
    )(buckets, residual, gain)


def fetch_kernel(w_hbm, out_ref, sem):
    copy = pltpu.make_async_copy(w_hbm.at[pl.ds(0, out_ref.shape[0])], out_ref, sem)
    copy.start()
    copy.wait()


def fetch(weight, count):
    return pl.pallas_call(
        fetch_kernel,
        in_specs=[pl.BlockSpec(memory_space=pltpu.HBM)],
        out_specs=pl.BlockSpec(memory_space=VMEM),
        out_shape=jax.ShapeDtypeStruct((count,) + weight.shape[1:], BF16),
        scratch_shapes=[pltpu.SemaphoreType.DMA],
        compiler_params=MOST,
        name="fetch",
    )(weight)


def gate_up_kernel(x_ref, w_ref, out_ref):
    hidden = w_ref.shape[2]
    tile = 256
    for i in range(2):
        for j in range(0, hidden, tile):
            part = jnp.dot(x_ref[...], w_ref[i, :, j : j + tile], preferred_element_type=F32)
            out_ref[:, i * hidden + j : i * hidden + j + tile] = part.astype(BF16)


def gate_up(x, weight):
    vm = pl.BlockSpec(memory_space=VMEM)
    return pl.pallas_call(
        gate_up_kernel,
        in_specs=[vm, vm],
        out_specs=vm,
        out_shape=jax.ShapeDtypeStruct((x.shape[0], 2 * weight.shape[2]), BF16),
        compiler_params=ROOM,
        name="gate_up",
    )(x, weight)


def down_kernel(x_ref, w_ref, out_ref):
    tile = 128
    for j in range(0, w_ref.shape[1], tile):
        out_ref[:, j : j + tile] = dot_nt(x_ref[...], w_ref[2, j : j + tile]).astype(BF16)


def down(x, weight):
    vm = pl.BlockSpec(memory_space=VMEM)
    return pl.pallas_call(
        down_kernel,
        in_specs=[vm, vm],
        out_specs=vm,
        out_shape=jax.ShapeDtypeStruct((x.shape[0], weight.shape[1]), BF16),
        compiler_params=ROOM,
        name="down",
    )(x, weight)


def combine_kernel(
    bucket_any, ids_ref, logits_ref, keep_ref, got_ref, out_ref, acc, bucket_ref, sem
):
    fetch_buckets = pltpu.make_async_copy(bucket_any, bucket_ref, sem)
    fetch_buckets.start()
    chips, rows, block = keep_ref.shape
    steps = ids_ref.shape[0]
    ids = jnp.concatenate([ids_ref[t] for t in range(steps)], axis=0)
    logits = jnp.concatenate([logits_ref[t] for t in range(steps)], axis=0)
    affinity = 1.0 / (1.0 + jnp.exp(-logits))
    weight = ROUTE_SCALE * affinity / jnp.sum(affinity, axis=1, keepdims=True)
    parity = lax.axis_index("ep") % 2
    col = lax.broadcasted_iota(jnp.int32, (rows, 2 * chips), 1)
    expert = jnp.where(col < chips, 2 * col + parity, 2 * (col - chips) + 1 - parity)
    share = jnp.zeros((rows, 2 * chips), F32)
    for k in range(ids.shape[1]):
        share = share + jnp.where(ids[:, k : k + 1] == expert, weight[:, k : k + 1], 0.0)
    acc[...] = jnp.zeros_like(acc)
    fetch_buckets.wait()
    for side, ref in enumerate((keep_ref, got_ref)):
        for c in range(chips):
            e = side * chips + c
            b = bucket_ref[e]
            acc[b] = acc[b] + share[:, e : e + 1] * ref[c].astype(F32)
    out_ref[...] = acc[...].astype(BF16)


def combine(buckets, ids, logits, keep, got, ranks):
    _, rows, block = keep.shape
    vm = pl.BlockSpec(memory_space=VMEM)
    return pl.pallas_call(
        combine_kernel,
        in_specs=[pl.BlockSpec(memory_space=pl.ANY), vm, vm, vm, vm],
        out_specs=vm,
        out_shape=jax.ShapeDtypeStruct((ranks, rows, block), BF16),
        scratch_shapes=[
            VMEM((ranks, rows, block), F32),
            SMEM(buckets.shape, jnp.int32),
            pltpu.SemaphoreType.DMA,
        ],
        compiler_params=ROOM,
        name="combine",
    )(buckets, ids, logits, keep, got)


def finish_kernel(part_ref, res_ref, out_ref):
    ranks, blocks, rows, block = part_ref.shape
    own = out_ref.shape[1]
    for b in range(blocks):
        x = res_ref[b, :rows].astype(F32)
        for r in range(ranks):
            x = x + part_ref[r, b].astype(F32)
        for t in range(out_ref.shape[0]):
            row = x[t * own : (t + 1) * own].astype(BF16)
            out_ref[t, :, b * block : (b + 1) * block] = row


def finish(parts, residual, steps, own):
    _, blocks, _, block = parts.shape
    vm = pl.BlockSpec(memory_space=VMEM)
    return pl.pallas_call(
        finish_kernel,
        in_specs=[vm, vm],
        out_specs=vm,
        out_shape=jax.ShapeDtypeStruct((steps, own, blocks * block), BF16),
        compiler_params=ROOM,
        name="finish",
    )(parts, residual)


def on_device(
    hidden_in,
    queries,
    new_keys,
    new_values,
    cache_keys,
    cache_values,
    cache_lengths,
    expert_ids,
    router_logits,
    norm_gain,
    out_sectioned,
    expert_sectioned,
    bucket_owner,
):
    steps, own_rows, width = hidden_in.shape
    n_ep = lax.axis_size("ep")
    n_rep = lax.axis_size("rep")
    chips = n_ep // 2
    block = width // n_rep
    mine = own_rows * steps
    rank = lax.axis_index("rep")
    pair = [(j, j ^ 1) for j in range(n_ep)]
    cores = [[j for j in range(n_ep) if j % 2 == k] for k in range(2)]

    def swap(x):
        return lax.ppermute(x, "ep", pair)

    def across(x):
        return lax.all_to_all(x, "ep", 0, 0, tiled=True, axis_index_groups=cores)

    def over_rep(x):
        return lax.all_to_all(x, "rep", 0, 0, tiled=True)

    keep, send = attention(
        bucket_owner,
        queries,
        new_keys,
        new_values,
        cache_keys,
        cache_values,
        cache_lengths[None],
        out_sectioned,
        chips,
    )
    own_block = lax.dynamic_slice_in_dim(hidden_in, rank * block, block, 2).reshape(mine, block)
    both = (keep.astype(F32) + swap(send).astype(F32)).astype(BF16)
    both, own_block = lax.optimization_barrier((both, own_block))
    parts = across(both)
    buckets = parts[:, 0, block : block + 2].astype(jnp.int32).T
    own_buckets, buckets = buckets[0], buckets.reshape(-1)
    residual = jnp.sum(parts[:, :, :block].astype(F32), axis=0) + own_block.astype(F32)
    residual = residual.astype(BF16)
    weight = jnp.transpose(expert_sectioned[0], (1, 0, 2))
    residual, weight = lax.optimization_barrier((residual, weight))
    other = swap(residual)
    into = fetch(weight, 2)
    other, into, own_buckets, buckets = lax.optimization_barrier(
        (other, into, own_buckets, buckets)
    )
    residual = jnp.concatenate([residual, other], axis=0)
    residual = over_rep(jnp.broadcast_to(residual, (n_rep,) + residual.shape))
    chosen = select(own_buckets, residual, norm_gain.reshape(1, width))
    arrivals = across(chosen).reshape(-1, block)
    hidden = weight.shape[2]
    partial = gate_up(arrivals, into)
    partial = over_rep(partial.reshape(n_rep, -1, 2 * hidden))
    partial = jnp.sum(partial.astype(F32), axis=0)
    activated = (jax.nn.silu(partial[:, :hidden]) * partial[:, hidden:]).astype(BF16)
    activated = over_rep(jnp.broadcast_to(activated, (n_rep,) + activated.shape))
    result = down(activated.reshape(-1, hidden), weight)
    back = across(result.reshape(chips, 2 * mine, block))
    routed = combine(
        buckets, expert_ids, router_logits, back[:, :mine], swap(back[:, mine:]), n_rep
    )
    near = [(j, j ^ 1) for j in range(n_rep)]
    lines = [[j for j in range(n_rep) if j % 2 == k] for k in range(2)]
    routed = (routed.astype(F32) + lax.ppermute(routed, "rep", near).astype(F32)).astype(BF16)
    routed = jnp.broadcast_to(routed, (n_rep // 2,) + routed.shape)
    routed = lax.all_to_all(routed, "rep", 0, 0, tiled=True, axis_index_groups=lines)
    return finish(routed, residual, steps, own_rows)


def solution(mesh):
    return jax.shard_map(
        on_device,
        mesh=mesh,
        in_specs=(
            P(None, "ep", None),
            P(None, None, "ep"),
            P(None, None, "ep"),
            P(None, None, "ep"),
            P(None, None, "ep"),
            P(None, None, "ep"),
            P(),
            P(None, "ep", None),
            P(None, "ep", None),
            P(),
            P("ep", "rep"),
            P("ep", "rep", None, None),
            P("ep", None),
        ),
        out_specs=P(None, "ep", None),
        check_vma=False,
    )
```

```python
import math

import jax
import jax.numpy as jnp
from jax import lax
from jax.experimental import pallas as pl
from jax.experimental.pallas import tpu as pltpu
from jax.sharding import PartitionSpec as P

DH = 128
ROUTE_SCALE = 2.827
EPSILON = 1e-06
GROUP = 16
NEVER = -1e30
VMEM = pltpu.VMEM
SMEM = pltpu.SMEM
F32 = jnp.float32
BF16 = jnp.bfloat16
MIB = 1024 * 1024
ROOM = pltpu.CompilerParams(vmem_limit_bytes=16 * MIB)
MOST = pltpu.CompilerParams(vmem_limit_bytes=49 * MIB)
FETCH = pltpu.CompilerParams(vmem_limit_bytes=58 * MIB)


def dot_nt(a, b):
    return lax.dot_general(a, b, (((1,), (1,)), ((), ())), preferred_element_type=F32)


def attention_kernel(
    owner_hbm,
    len_hbm,
    q_hbm,
    kn_hbm,
    vn_hbm,
    ck_hbm,
    cv_hbm,
    out_hbm,
    keep_ref,
    send_ref,
    owner_ref,
    len_ref,
    q_ref,
    kn_ref,
    vn_ref,
    ck_ref,
    cv_ref,
    out_ref,
    heads,
    sems,
):
    steps, rows, width = q_hbm.shape
    cached = ck_hbm.shape[1]
    groups = rows // GROUP
    fresh = [
        pltpu.make_async_copy(src, dst, sems.at[i])
        for i, (src, dst) in enumerate(
            ((q_hbm, q_ref), (kn_hbm, kn_ref), (vn_hbm, vn_ref), (out_hbm, out_ref))
        )
    ]
    small = [
        pltpu.make_async_copy(len_hbm, len_ref, sems.at[8]),
        pltpu.make_async_copy(owner_hbm, owner_ref, sems.at[9]),
    ]
    old = []
    for g in range(2):
        part = pl.ds(g * (rows // 2), rows // 2)
        for i, (src, dst) in enumerate(((ck_hbm, ck_ref), (cv_hbm, cv_ref))):
            sem = sems.at[4 + 2 * g + i]
            old.append(pltpu.make_async_copy(src.at[part], dst.at[part], sem))
    for copy in fresh[:3] + old[:1] + small + old[1:] + fresh[3:]:
        copy.start()
    parity = lax.axis_index("ep") % 2
    m = steps * GROUP
    n = GROUP * cached
    factor = 1.0 / math.sqrt(DH)
    row = lax.broadcasted_iota(jnp.int32, (m, n), 0)
    col = lax.broadcasted_iota(jnp.int32, (m, n), 1)
    own = col // cached == row % GROUP
    place = col % cached
    row = lax.broadcasted_iota(jnp.int32, (m, m), 0)
    col = lax.broadcasted_iota(jnp.int32, (m, m), 1)
    recent = (col % GROUP == row % GROUP) & (col // GROUP <= row // GROUP)
    row = lax.broadcasted_iota(jnp.int32, (m, rows), 0)
    col = lax.broadcasted_iota(jnp.int32, (m, rows), 1)
    for copy in fresh[:3] + small[:1]:
        copy.wait()
    lengths = len_ref[...].astype(F32)
    def score(g, h, live):
        part = slice(g * GROUP, (g + 1) * GROUP)
        cut = slice(h * DH, (h + 1) * DH)
        q = q_ref[:, part, cut].reshape(m, DH)
        so = dot_nt(q, ck_ref[part, :, cut].reshape(n, DH)) * factor
        sn = dot_nt(q, kn_ref[:, part, cut].reshape(m, DH)) * factor
        return jnp.where(live, so, NEVER), jnp.where(recent, sn, NEVER)

    def soften(so, sn):
        top = jnp.maximum(jnp.max(so, axis=1, keepdims=True), jnp.max(sn, axis=1, keepdims=True))
        eo = jnp.exp(so - top)
        en = jnp.exp(sn - top)
        total = jnp.sum(eo, axis=1, keepdims=True) + jnp.sum(en, axis=1, keepdims=True)
        return eo.astype(BF16), en.astype(BF16), 1.0 / total

    def gather(g, h, eo, en, inverse):
        part = slice(g * GROUP, (g + 1) * GROUP)
        cut = slice(h * DH, (h + 1) * DH)
        w = jnp.dot(
            eo, cv_ref[part, :, cut].reshape(n, DH), preferred_element_type=F32
        ) + jnp.dot(en, vn_ref[:, part, cut].reshape(m, DH), preferred_element_type=F32)
        return (w * inverse).astype(BF16).reshape(steps, GROUP, DH)

    scores = []
    for g in range(groups):
        if g % (groups // 2) == 0:
            for copy in old[g : g + 2]:
                copy.wait()
        length = jnp.sum(
            jnp.where(col == row % GROUP + g * GROUP, lengths, 0.0), axis=1, keepdims=True
        )
        live = own & (place < length.astype(jnp.int32))
        scores += [(g, h, *score(g, h, live)) for h in range(width // DH)]
    soft = [(g, h, *soften(so, sn)) for g, h, so, sn in scores]
    for g, h, *rest in soft:
        part = slice(g * GROUP, (g + 1) * GROUP)
        heads[:, part, h * DH : (h + 1) * DH] = gather(g, h, *rest)
    every = steps * rows
    half = every // 2
    mine = keep_ref.shape[1]
    own_rows = mine // steps
    j = lax.broadcasted_iota(jnp.int32, (every, 1), 0)
    core = jnp.where(j < half, parity, 1 - parity)
    chip = (j % half) // mine
    step = (j % mine) // own_rows
    wanted = step * rows + (chip * 2 + core) * own_rows + j % own_rows
    source = lax.broadcasted_iota(jnp.int32, (every, every), 1)
    order = jnp.where(source == wanted, 1.0, 0.0).astype(BF16)
    h = jnp.dot(order, heads[...].reshape(every, width), preferred_element_type=F32)
    h = h.astype(BF16)
    small[1].wait()
    rank = lax.axis_index("rep")
    bucket = jnp.int32(0)
    for b in range(owner_ref.shape[1]):
        bucket = jnp.where(owner_ref[0, b] == rank, b, bucket)
    fresh[3].wait()
    block = out_ref.shape[1]
    chips = half // mine
    for side, ref in enumerate((keep_ref, send_ref)):
        part = jnp.dot(
            h[side * half : (side + 1) * half], out_ref[...], preferred_element_type=F32
        )
        ref[:, :, :block] = part.astype(BF16).reshape(chips, mine, block)
        lane = lax.broadcasted_iota(jnp.int32, (chips, mine, ref.shape[2] - block), 2)
        ref[:, :, block:] = jnp.where(lane == side, bucket, 0).astype(F32).astype(BF16)


def attention(owner, queries, new_keys, new_values, cache_keys, cache_values, lengths, out, chips):
    steps, rows, width = queries.shape
    mine = steps * rows // (2 * chips)
    shape = (chips, mine, out.shape[1] + 128)
    vm = pl.BlockSpec(memory_space=VMEM)
    hbm = pl.BlockSpec(memory_space=pltpu.HBM)
    operands = (queries, new_keys, new_values, cache_keys, cache_values, out)
    return pl.pallas_call(
        attention_kernel,
        in_specs=[hbm] * (2 + len(operands)),
        out_specs=[vm, vm],
        out_shape=[jax.ShapeDtypeStruct(shape, BF16)] * 2,
        scratch_shapes=[SMEM(owner.shape, jnp.int32), VMEM(lengths.shape, jnp.int32)]
        + [VMEM(x.shape, BF16) for x in operands]
        + [
            VMEM((steps, rows, width), BF16),
            pltpu.SemaphoreType.DMA((10,)),
        ],
        compiler_params=FETCH,
        name="attention",
    )(owner, lengths, *operands)


def select_kernel(bucket_any, res_ref, gain_ref, out_ref, norm, bucket_ref, sem):
    fetch_buckets = pltpu.make_async_copy(bucket_any, bucket_ref, sem)
    fetch_buckets.start()
    blocks, rows, block = res_ref.shape
    total = jnp.zeros((rows, block), F32)
    for b in range(blocks):
        x = res_ref[b].astype(F32)
        total = total + x * x
    mean = jnp.sum(total, axis=1, keepdims=True) / (blocks * block)
    scale = lax.rsqrt(mean + EPSILON)
    for b in range(blocks):
        gain = gain_ref[:, b * block : (b + 1) * block]
        norm[b] = (res_ref[b].astype(F32) * scale * gain).astype(BF16)
    fetch_buckets.wait()
    for c in range(out_ref.shape[0]):
        out_ref[c] = norm[bucket_ref[c]]


def select(buckets, residual, gain):
    blocks, rows, block = residual.shape
    chips = buckets.shape[0]
    vm = pl.BlockSpec(memory_space=VMEM)
    return pl.pallas_call(
        select_kernel,
        in_specs=[pl.BlockSpec(memory_space=pl.ANY), vm, vm],
        out_specs=vm,
        out_shape=jax.ShapeDtypeStruct((chips, rows, block), BF16),
        scratch_shapes=[
            VMEM(residual.shape, BF16),
            SMEM(buckets.shape, jnp.int32),
            pltpu.SemaphoreType.DMA,
        ],
        compiler_params=ROOM,
        name="select",
    )(buckets, residual, gain)


def fetch_kernel(w_hbm, out_ref, sem):
    copy = pltpu.make_async_copy(w_hbm.at[pl.ds(0, out_ref.shape[0])], out_ref, sem)
    copy.start()
    copy.wait()


def fetch(weight, count):
    return pl.pallas_call(
        fetch_kernel,
        in_specs=[pl.BlockSpec(memory_space=pltpu.HBM)],
        out_specs=pl.BlockSpec(memory_space=VMEM),
        out_shape=jax.ShapeDtypeStruct((count,) + weight.shape[1:], BF16),
        scratch_shapes=[pltpu.SemaphoreType.DMA],
        compiler_params=MOST,
        name="fetch",
    )(weight)


def gate_up_kernel(x_ref, w_ref, out_ref):
    hidden = w_ref.shape[2]
    tile = 256
    for i in range(2):
        for j in range(0, hidden, tile):
            part = jnp.dot(x_ref[...], w_ref[i, :, j : j + tile], preferred_element_type=F32)
            out_ref[:, i * hidden + j : i * hidden + j + tile] = part.astype(BF16)


def gate_up(x, weight):
    vm = pl.BlockSpec(memory_space=VMEM)
    return pl.pallas_call(
        gate_up_kernel,
        in_specs=[vm, vm],
        out_specs=vm,
        out_shape=jax.ShapeDtypeStruct((x.shape[0], 2 * weight.shape[2]), BF16),
        compiler_params=ROOM,
        name="gate_up",
    )(x, weight)


def down_kernel(x_ref, w_ref, out_ref):
    tile = 128
    for j in range(0, w_ref.shape[1], tile):
        out_ref[:, j : j + tile] = dot_nt(x_ref[...], w_ref[2, j : j + tile]).astype(BF16)


def down(x, weight):
    vm = pl.BlockSpec(memory_space=VMEM)
    return pl.pallas_call(
        down_kernel,
        in_specs=[vm, vm],
        out_specs=vm,
        out_shape=jax.ShapeDtypeStruct((x.shape[0], weight.shape[1]), BF16),
        compiler_params=ROOM,
        name="down",
    )(x, weight)


def combine_kernel(
    bucket_any, ids_ref, logits_ref, keep_ref, got_ref, low_ref, high_ref, acc, bucket_ref, sem
):
    fetch_buckets = pltpu.make_async_copy(bucket_any, bucket_ref, sem)
    fetch_buckets.start()
    chips, rows, block = keep_ref.shape
    steps = ids_ref.shape[0]
    ids = jnp.concatenate([ids_ref[t] for t in range(steps)], axis=0)
    logits = jnp.concatenate([logits_ref[t] for t in range(steps)], axis=0)
    affinity = 1.0 / (1.0 + jnp.exp(-logits))
    weight = ROUTE_SCALE * affinity / jnp.sum(affinity, axis=1, keepdims=True)
    parity = lax.axis_index("ep") % 2
    col = lax.broadcasted_iota(jnp.int32, (rows, 2 * chips), 1)
    expert = jnp.where(col < chips, 2 * col + parity, 2 * (col - chips) + 1 - parity)
    share = jnp.zeros((rows, 2 * chips), F32)
    for k in range(ids.shape[1]):
        share = share + jnp.where(ids[:, k : k + 1] == expert, weight[:, k : k + 1], 0.0)
    acc[...] = jnp.zeros_like(acc)
    fetch_buckets.wait()
    for side, ref in enumerate((keep_ref, got_ref)):
        for c in range(chips):
            e = side * chips + c
            b = bucket_ref[e]
            acc[b] = acc[b] + share[:, e : e + 1] * ref[c].astype(F32)
    half = low_ref.shape[0]
    low_ref[...] = acc[:half].astype(BF16)
    high_ref[...] = acc[half:].astype(BF16)


def combine(buckets, ids, logits, keep, got, ranks):
    _, rows, block = keep.shape
    vm = pl.BlockSpec(memory_space=VMEM)
    return pl.pallas_call(
        combine_kernel,
        in_specs=[pl.BlockSpec(memory_space=pl.ANY), vm, vm, vm, vm],
        out_specs=[vm, vm],
        out_shape=[jax.ShapeDtypeStruct((ranks // 2, rows, block), BF16)] * 2,
        scratch_shapes=[
            VMEM((ranks, rows, block), F32),
            SMEM(buckets.shape, jnp.int32),
            pltpu.SemaphoreType.DMA,
        ],
        compiler_params=ROOM,
        name="combine",
    )(buckets, ids, logits, keep, got)


def finish_kernel(low_ref, high_ref, res_ref, out_ref):
    half, rows, block = low_ref.shape
    own = out_ref.shape[1]
    for b in range(2 * half):
        part = low_ref[b] if b < half else high_ref[b - half]
        x = res_ref[b, :rows].astype(F32) + part.astype(F32)
        for t in range(out_ref.shape[0]):
            row = x[t * own : (t + 1) * own].astype(BF16)
            out_ref[t, :, b * block : (b + 1) * block] = row


def finish(low, high, residual, steps, own):
    blocks, _, block = residual.shape
    vm = pl.BlockSpec(memory_space=VMEM)
    return pl.pallas_call(
        finish_kernel,
        in_specs=[vm, vm, vm],
        out_specs=vm,
        out_shape=jax.ShapeDtypeStruct((steps, own, blocks * block), BF16),
        compiler_params=ROOM,
        name="finish",
    )(low, high, residual)


def on_device(
    hidden_in,
    queries,
    new_keys,
    new_values,
    cache_keys,
    cache_values,
    cache_lengths,
    expert_ids,
    router_logits,
    norm_gain,
    out_sectioned,
    expert_sectioned,
    bucket_owner,
):
    steps, own_rows, width = hidden_in.shape
    n_ep = lax.axis_size("ep")
    n_rep = lax.axis_size("rep")
    chips = n_ep // 2
    block = width // n_rep
    mine = own_rows * steps
    rank = lax.axis_index("rep")
    pair = [(j, j ^ 1) for j in range(n_ep)]
    cores = [[j for j in range(n_ep) if j % 2 == k] for k in range(2)]

    def swap(x):
        return lax.ppermute(x, "ep", pair)

    def across(x):
        return lax.all_to_all(x, "ep", 0, 0, tiled=True, axis_index_groups=cores)

    def over_rep(x):
        return lax.all_to_all(x, "rep", 0, 0, tiled=True)

    keep, send = attention(
        bucket_owner,
        queries,
        new_keys,
        new_values,
        cache_keys,
        cache_values,
        cache_lengths[None],
        out_sectioned,
        chips,
    )
    own_block = lax.dynamic_slice_in_dim(hidden_in, rank * block, block, 2).reshape(mine, block)
    both = (keep.astype(F32) + swap(send).astype(F32)).astype(BF16)
    both, own_block = lax.optimization_barrier((both, own_block))
    parts = across(both)
    buckets = parts[:, 0, block : block + 2].astype(jnp.int32).T
    own_buckets, buckets = buckets[0], buckets.reshape(-1)
    residual = jnp.sum(parts[:, :, :block].astype(F32), axis=0) + own_block.astype(F32)
    residual = residual.astype(BF16)
    weight = jnp.transpose(expert_sectioned[0], (1, 0, 2))
    residual, weight = lax.optimization_barrier((residual, weight))
    other = swap(residual)
    into = fetch(weight, 2)
    other, into, own_buckets, buckets = lax.optimization_barrier(
        (other, into, own_buckets, buckets)
    )
    residual = jnp.concatenate([residual, other], axis=0)
    residual = over_rep(jnp.broadcast_to(residual, (n_rep,) + residual.shape))
    chosen = select(own_buckets, residual, norm_gain.reshape(1, width))
    arrivals = across(chosen).reshape(-1, block)
    hidden = weight.shape[2]
    partial = gate_up(arrivals, into)
    partial = over_rep(partial.reshape(n_rep, -1, 2 * hidden))
    partial = jnp.sum(partial.astype(F32), axis=0)
    activated = (jax.nn.silu(partial[:, :hidden]) * partial[:, hidden:]).astype(BF16)
    activated = over_rep(jnp.broadcast_to(activated, (n_rep,) + activated.shape))
    result = down(activated.reshape(-1, hidden), weight)
    back = across(result.reshape(chips, 2 * mine, block))
    low, high = combine(
        buckets, expert_ids, router_logits, back[:, :mine], swap(back[:, mine:]), n_rep
    )
    lines = n_rep // 2
    turns = (
        [(j, j ^ 1) for j in range(n_rep)],
        [(j, j ^ 2) for j in range(n_rep)],
        [(j, ((j // 2 + (1 if j // 2 % 2 else -1)) % lines) * 2 + j % 2) for j in range(n_rep)],
    )
    def add(x, turn):
        return (x.astype(F32) + lax.ppermute(x, "rep", turn).astype(F32)).astype(BF16)

    for i in range(3):
        low, high = add(low, turns[i]), add(high, turns[(i + 1) % 3])
    return finish(low, high, residual, steps, own_rows)


def solution(mesh):
    return jax.shard_map(
        on_device,
        mesh=mesh,
        in_specs=(
            P(None, "ep", None),
            P(None, None, "ep"),
            P(None, None, "ep"),
            P(None, None, "ep"),
            P(None, None, "ep"),
            P(None, None, "ep"),
            P(),
            P(None, "ep", None),
            P(None, "ep", None),
            P(),
            P("ep", "rep"),
            P("ep", "rep", None, None),
            P("ep", None),
        ),
        out_specs=P(None, "ep", None),
        check_vma=False,
    )
```

```python
import functools
import math

import jax
import jax.numpy as jnp
from jax import lax
from jax.experimental import pallas as pl
from jax.experimental.pallas import tpu as pltpu
from jax.sharding import PartitionSpec as P

DH = 128
ROUTE_SCALE = 2.827
EPSILON = 1e-06
GROUP = 16
NEVER = -1e30
VMEM = pltpu.VMEM
SMEM = pltpu.SMEM
F32 = jnp.float32
BF16 = jnp.bfloat16
MIB = 1024 * 1024
ROOM = pltpu.CompilerParams(vmem_limit_bytes=16 * MIB)
MOST = pltpu.CompilerParams(vmem_limit_bytes=49 * MIB)
FETCH = pltpu.CompilerParams(vmem_limit_bytes=58 * MIB)


def dot_nt(a, b):
    return lax.dot_general(a, b, (((1,), (1,)), ((), ())), preferred_element_type=F32)


def attention_kernel(
    owner_hbm,
    len_hbm,
    q_hbm,
    kn_hbm,
    vn_hbm,
    ck_hbm,
    cv_hbm,
    out_hbm,
    keep_ref,
    send_ref,
    owner_ref,
    len_ref,
    q_ref,
    kn_ref,
    vn_ref,
    ck_ref,
    cv_ref,
    out_ref,
    heads,
    sems,
):
    steps, rows, width = q_hbm.shape
    cached = ck_hbm.shape[1]
    groups = rows // GROUP
    fresh = [
        pltpu.make_async_copy(src, dst, sems.at[i])
        for i, (src, dst) in enumerate(
            ((q_hbm, q_ref), (kn_hbm, kn_ref), (vn_hbm, vn_ref), (out_hbm, out_ref))
        )
    ]
    small = [
        pltpu.make_async_copy(len_hbm, len_ref, sems.at[8]),
        pltpu.make_async_copy(owner_hbm, owner_ref, sems.at[9]),
    ]
    old = []
    for g in range(2):
        part = pl.ds(g * (rows // 2), rows // 2)
        for i, (src, dst) in enumerate(((ck_hbm, ck_ref), (cv_hbm, cv_ref))):
            sem = sems.at[4 + 2 * g + i]
            old.append(pltpu.make_async_copy(src.at[part], dst.at[part], sem))
    for copy in fresh[:3] + old[:1] + small + old[1:] + fresh[3:]:
        copy.start()
    parity = lax.axis_index("ep") % 2
    m = steps * GROUP
    n = GROUP * cached
    factor = 1.0 / math.sqrt(DH)
    row = lax.broadcasted_iota(jnp.int32, (m, n), 0)
    col = lax.broadcasted_iota(jnp.int32, (m, n), 1)
    own = col // cached == row % GROUP
    place = col % cached
    row = lax.broadcasted_iota(jnp.int32, (m, m), 0)
    col = lax.broadcasted_iota(jnp.int32, (m, m), 1)
    recent = (col % GROUP == row % GROUP) & (col // GROUP <= row // GROUP)
    row = lax.broadcasted_iota(jnp.int32, (m, rows), 0)
    col = lax.broadcasted_iota(jnp.int32, (m, rows), 1)
    for copy in fresh[:3] + small[:1]:
        copy.wait()
    lengths = len_ref[...].astype(F32)
    def score(g, h, live):
        part = slice(g * GROUP, (g + 1) * GROUP)
        cut = slice(h * DH, (h + 1) * DH)
        q = q_ref[:, part, cut].reshape(m, DH)
        so = dot_nt(q, ck_ref[part, :, cut].reshape(n, DH)) * factor
        sn = dot_nt(q, kn_ref[:, part, cut].reshape(m, DH)) * factor
        return jnp.where(live, so, NEVER), jnp.where(recent, sn, NEVER)

    def soften(so, sn):
        top = jnp.maximum(jnp.max(so, axis=1, keepdims=True), jnp.max(sn, axis=1, keepdims=True))
        eo = jnp.exp(so - top)
        en = jnp.exp(sn - top)
        total = jnp.sum(eo, axis=1, keepdims=True) + jnp.sum(en, axis=1, keepdims=True)
        return eo.astype(BF16), en.astype(BF16), 1.0 / total

    def gather(g, h, eo, en, inverse):
        part = slice(g * GROUP, (g + 1) * GROUP)
        cut = slice(h * DH, (h + 1) * DH)
        w = jnp.dot(
            eo, cv_ref[part, :, cut].reshape(n, DH), preferred_element_type=F32
        ) + jnp.dot(en, vn_ref[:, part, cut].reshape(m, DH), preferred_element_type=F32)
        return (w * inverse).astype(BF16).reshape(steps, GROUP, DH)

    scores = []
    for g in range(groups):
        if g % (groups // 2) == 0:
            for copy in old[g : g + 2]:
                copy.wait()
        length = jnp.sum(
            jnp.where(col == row % GROUP + g * GROUP, lengths, 0.0), axis=1, keepdims=True
        )
        live = own & (place < length.astype(jnp.int32))
        scores += [(g, h, *score(g, h, live)) for h in range(width // DH)]
    soft = [(g, h, *soften(so, sn)) for g, h, so, sn in scores]
    for g, h, *rest in soft:
        part = slice(g * GROUP, (g + 1) * GROUP)
        heads[:, part, h * DH : (h + 1) * DH] = gather(g, h, *rest)
    every = steps * rows
    half = every // 2
    mine = keep_ref.shape[1]
    own_rows = mine // steps
    j = lax.broadcasted_iota(jnp.int32, (every, 1), 0)
    core = jnp.where(j < half, parity, 1 - parity)
    chip = (j % half) // mine
    step = (j % mine) // own_rows
    wanted = step * rows + (chip * 2 + core) * own_rows + j % own_rows
    source = lax.broadcasted_iota(jnp.int32, (every, every), 1)
    order = jnp.where(source == wanted, 1.0, 0.0).astype(BF16)
    h = jnp.dot(order, heads[...].reshape(every, width), preferred_element_type=F32)
    h = h.astype(BF16)
    small[1].wait()
    rank = lax.axis_index("rep")
    bucket = jnp.int32(0)
    for b in range(owner_ref.shape[1]):
        bucket = jnp.where(owner_ref[0, b] == rank, b, bucket)
    fresh[3].wait()
    block = out_ref.shape[1]
    chips = half // mine
    for side, ref in enumerate((keep_ref, send_ref)):
        part = jnp.dot(
            h[side * half : (side + 1) * half], out_ref[...], preferred_element_type=F32
        )
        ref[:, :, :block] = part.astype(BF16).reshape(chips, mine, block)
        lane = lax.broadcasted_iota(jnp.int32, (chips, mine, ref.shape[2] - block), 2)
        ref[:, :, block:] = jnp.where(lane == side, bucket, 0).astype(F32).astype(BF16)


def attention(owner, queries, new_keys, new_values, cache_keys, cache_values, lengths, out, chips):
    steps, rows, width = queries.shape
    mine = steps * rows // (2 * chips)
    shape = (chips, mine, out.shape[1] + 128)
    vm = pl.BlockSpec(memory_space=VMEM)
    hbm = pl.BlockSpec(memory_space=pltpu.HBM)
    operands = (queries, new_keys, new_values, cache_keys, cache_values, out)
    return pl.pallas_call(
        attention_kernel,
        in_specs=[hbm] * (2 + len(operands)),
        out_specs=[vm, vm],
        out_shape=[jax.ShapeDtypeStruct(shape, BF16)] * 2,
        scratch_shapes=[SMEM(owner.shape, jnp.int32), VMEM(lengths.shape, jnp.int32)]
        + [VMEM(x.shape, BF16) for x in operands]
        + [
            VMEM((steps, rows, width), BF16),
            pltpu.SemaphoreType.DMA((10,)),
        ],
        compiler_params=FETCH,
        name="attention",
    )(owner, lengths, *operands)


def select_kernel(bucket_any, res_ref, gain_ref, out_ref, norm, bucket_ref, sem):
    fetch_buckets = pltpu.make_async_copy(bucket_any, bucket_ref, sem)
    fetch_buckets.start()
    blocks, rows, block = res_ref.shape
    total = jnp.zeros((rows, block), F32)
    for b in range(blocks):
        x = res_ref[b].astype(F32)
        total = total + x * x
    mean = jnp.sum(total, axis=1, keepdims=True) / (blocks * block)
    scale = lax.rsqrt(mean + EPSILON)
    for b in range(blocks):
        gain = gain_ref[:, b * block : (b + 1) * block]
        norm[b] = (res_ref[b].astype(F32) * scale * gain).astype(BF16)
    fetch_buckets.wait()
    for c in range(out_ref.shape[0]):
        out_ref[c] = norm[bucket_ref[c]]


def select(buckets, residual, gain):
    blocks, rows, block = residual.shape
    chips = buckets.shape[0]
    vm = pl.BlockSpec(memory_space=VMEM)
    return pl.pallas_call(
        select_kernel,
        in_specs=[pl.BlockSpec(memory_space=pl.ANY), vm, vm],
        out_specs=vm,
        out_shape=jax.ShapeDtypeStruct((chips, rows, block), BF16),
        scratch_shapes=[
            VMEM(residual.shape, BF16),
            SMEM(buckets.shape, jnp.int32),
            pltpu.SemaphoreType.DMA,
        ],
        compiler_params=ROOM,
        name="select",
    )(buckets, residual, gain)


def fetch_kernel(w_hbm, out_ref, sem):
    copy = pltpu.make_async_copy(w_hbm.at[pl.ds(0, out_ref.shape[0])], out_ref, sem)
    copy.start()
    copy.wait()


def fetch(weight, count):
    return pl.pallas_call(
        fetch_kernel,
        in_specs=[pl.BlockSpec(memory_space=pltpu.HBM)],
        out_specs=pl.BlockSpec(memory_space=VMEM),
        out_shape=jax.ShapeDtypeStruct((count,) + weight.shape[1:], BF16),
        scratch_shapes=[pltpu.SemaphoreType.DMA],
        compiler_params=MOST,
        name="fetch",
    )(weight)


def gate_up_kernel(x_ref, w_ref, out_ref):
    hidden = w_ref.shape[2]
    tile = 256
    for i in range(2):
        for j in range(0, hidden, tile):
            part = jnp.dot(x_ref[...], w_ref[i, :, j : j + tile], preferred_element_type=F32)
            out_ref[:, i * hidden + j : i * hidden + j + tile] = part.astype(BF16)


def gate_up(x, weight):
    vm = pl.BlockSpec(memory_space=VMEM)
    return pl.pallas_call(
        gate_up_kernel,
        in_specs=[vm, vm],
        out_specs=vm,
        out_shape=jax.ShapeDtypeStruct((x.shape[0], 2 * weight.shape[2]), BF16),
        compiler_params=ROOM,
        name="gate_up",
    )(x, weight)


def down_kernel(x_ref, w_ref, out_ref):
    tile = 128
    for j in range(0, w_ref.shape[1], tile):
        out_ref[:, j : j + tile] = dot_nt(x_ref[...], w_ref[2, j : j + tile]).astype(BF16)


def down(x, weight):
    vm = pl.BlockSpec(memory_space=VMEM)
    return pl.pallas_call(
        down_kernel,
        in_specs=[vm, vm],
        out_specs=vm,
        out_shape=jax.ShapeDtypeStruct((x.shape[0], weight.shape[1]), BF16),
        compiler_params=ROOM,
        name="down",
    )(x, weight)


def combine_kernel(side, bucket_any, ids_ref, logits_ref, part_ref, *rest):
    *given, bucket_ref, sem = rest
    fetch_buckets = pltpu.make_async_copy(bucket_any, bucket_ref, sem)
    fetch_buckets.start()
    chips, rows, block = part_ref.shape
    steps = ids_ref.shape[0]
    ids = jnp.concatenate([ids_ref[t] for t in range(steps)], axis=0)
    logits = jnp.concatenate([logits_ref[t] for t in range(steps)], axis=0)
    affinity = 1.0 / (1.0 + jnp.exp(-logits))
    weight = ROUTE_SCALE * affinity / jnp.sum(affinity, axis=1, keepdims=True)
    parity = lax.axis_index("ep") % 2
    core = parity if side == 0 else 1 - parity
    expert = 2 * lax.broadcasted_iota(jnp.int32, (rows, chips), 1) + core
    share = jnp.zeros((rows, chips), F32)
    for k in range(ids.shape[1]):
        share = share + jnp.where(ids[:, k : k + 1] == expert, weight[:, k : k + 1], 0.0)
    if side == 0:
        (acc,) = given
        acc[...] = jnp.zeros_like(acc)
    else:
        start_ref, low_ref, high_ref, acc = given
        acc[...] = start_ref[...]
    fetch_buckets.wait()
    for c in range(chips):
        b = bucket_ref[side * chips + c]
        acc[b] = acc[b] + share[:, c : c + 1] * part_ref[c].astype(F32)
    if side == 1:
        half = low_ref.shape[0]
        low_ref[...] = acc[:half].astype(BF16)
        high_ref[...] = acc[half:].astype(BF16)


def combine(buckets, ids, logits, part, ranks, start=None):
    _, rows, block = part.shape
    vm = pl.BlockSpec(memory_space=VMEM)
    shape = (ranks, rows, block)
    small = [SMEM(buckets.shape, jnp.int32), pltpu.SemaphoreType.DMA]
    if start is None:
        side, operands, scratch = 0, (ids, logits, part), small
        out_shape = [jax.ShapeDtypeStruct(shape, F32)]
    else:
        side, operands, scratch = 1, (ids, logits, part, start), [VMEM(shape, F32)] + small
        out_shape = [jax.ShapeDtypeStruct((ranks // 2, rows, block), BF16)] * 2
    return pl.pallas_call(
        functools.partial(combine_kernel, side),
        in_specs=[pl.BlockSpec(memory_space=pl.ANY)] + [vm] * len(operands),
        out_specs=[vm] * len(out_shape),
        out_shape=out_shape,
        scratch_shapes=scratch,
        compiler_params=ROOM,
        name="combine",
    )(buckets, *operands)


def finish_kernel(low_ref, high_ref, res_ref, out_ref):
    half, rows, block = low_ref.shape
    own = out_ref.shape[1]
    for b in range(2 * half):
        part = low_ref[b] if b < half else high_ref[b - half]
        x = res_ref[b].astype(F32)[:rows] + part.astype(F32)
        for t in range(out_ref.shape[0]):
            row = x[t * own : (t + 1) * own].astype(BF16)
            out_ref[t, :, b * block : (b + 1) * block] = row


def finish(low, high, residual, steps, own):
    blocks, _, block = residual.shape
    vm = pl.BlockSpec(memory_space=VMEM)
    return pl.pallas_call(
        finish_kernel,
        in_specs=[vm, vm, vm],
        out_specs=vm,
        out_shape=jax.ShapeDtypeStruct((steps, own, blocks * block), BF16),
        compiler_params=ROOM,
        name="finish",
    )(low, high, residual)


def on_device(
    hidden_in,
    queries,
    new_keys,
    new_values,
    cache_keys,
    cache_values,
    cache_lengths,
    expert_ids,
    router_logits,
    norm_gain,
    out_sectioned,
    expert_sectioned,
    bucket_owner,
):
    steps, own_rows, width = hidden_in.shape
    n_ep = lax.axis_size("ep")
    n_rep = lax.axis_size("rep")
    chips = n_ep // 2
    block = width // n_rep
    mine = own_rows * steps
    rank = lax.axis_index("rep")
    pair = [(j, j ^ 1) for j in range(n_ep)]
    cores = [[j for j in range(n_ep) if j % 2 == k] for k in range(2)]

    def swap(x):
        return lax.ppermute(x, "ep", pair)

    def across(x):
        return lax.all_to_all(x, "ep", 0, 0, tiled=True, axis_index_groups=cores)

    def over_rep(x):
        return lax.all_to_all(x, "rep", 0, 0, tiled=True)

    keep, send = attention(
        bucket_owner,
        queries,
        new_keys,
        new_values,
        cache_keys,
        cache_values,
        cache_lengths[None],
        out_sectioned,
        chips,
    )
    own_block = lax.dynamic_slice_in_dim(hidden_in, rank * block, block, 2).reshape(mine, block)
    both = (keep.astype(F32) + swap(send).astype(F32)).astype(BF16)
    both, own_block = lax.optimization_barrier((both, own_block))
    parts = across(both)
    buckets = parts[:, 0, block : block + 2].astype(jnp.int32).T
    own_buckets, buckets = buckets[0], buckets.reshape(-1)
    residual = jnp.sum(parts[:, :, :block].astype(F32), axis=0) + own_block.astype(F32)
    residual = residual.astype(BF16)
    weight = jnp.transpose(expert_sectioned[0], (1, 0, 2))
    residual, weight = lax.optimization_barrier((residual, weight))
    other = swap(residual)
    into = fetch(weight, 2)
    other, into, own_buckets, buckets = lax.optimization_barrier(
        (other, into, own_buckets, buckets)
    )
    residual = jnp.concatenate([residual, other], axis=0)
    residual = over_rep(jnp.broadcast_to(residual, (n_rep,) + residual.shape))
    chosen = select(own_buckets, residual, norm_gain.reshape(1, width))
    arrivals = across(chosen).reshape(-1, block)
    hidden = weight.shape[2]
    partial = gate_up(arrivals, into)
    partial = over_rep(partial.reshape(n_rep, -1, 2 * hidden))
    partial = jnp.sum(partial.astype(F32), axis=0)
    activated = (jax.nn.silu(partial[:, :hidden]) * partial[:, hidden:]).astype(BF16)
    activated = over_rep(jnp.broadcast_to(activated, (n_rep,) + activated.shape))
    result = down(activated.reshape(-1, hidden), weight)
    back = across(result.reshape(chips, 2 * mine, block))
    got = swap(back[:, mine:])
    (start,) = combine(buckets, expert_ids, router_logits, back[:, :mine], n_rep)
    low, high = combine(buckets, expert_ids, router_logits, got, n_rep, start)
    lines = n_rep // 2
    turns = (
        [(j, j ^ 1) for j in range(n_rep)],
        [(j, j ^ 2) for j in range(n_rep)],
        [(j, ((j // 2 + (1 if j // 2 % 2 else -1)) % lines) * 2 + j % 2) for j in range(n_rep)],
    )
    def add(x, turn):
        return (x.astype(F32) + lax.ppermute(x, "rep", turn).astype(F32)).astype(BF16)

    for i in range(3):
        low, high = add(low, turns[i]), add(high, turns[(i + 1) % 3])
    return finish(low, high, residual, steps, own_rows)


def solution(mesh):
    return jax.shard_map(
        on_device,
        mesh=mesh,
        in_specs=(
            P(None, "ep", None),
            P(None, None, "ep"),
            P(None, None, "ep"),
            P(None, None, "ep"),
            P(None, None, "ep"),
            P(None, None, "ep"),
            P(),
            P(None, "ep", None),
            P(None, "ep", None),
            P(),
            P("ep", "rep"),
            P("ep", "rep", None, None),
            P("ep", None),
        ),
        out_specs=P(None, "ep", None),
        check_vma=False,
    )
```

```python
import functools
import math

import jax
import jax.numpy as jnp
from jax import lax
from jax.experimental import pallas as pl
from jax.experimental.pallas import tpu as pltpu
from jax.sharding import PartitionSpec as P

DH = 128
ROUTE_SCALE = 2.827
EPSILON = 1e-06
GROUP = 16
NEVER = -1e30
VMEM = pltpu.VMEM
SMEM = pltpu.SMEM
F32 = jnp.float32
BF16 = jnp.bfloat16
MIB = 1024 * 1024
ROOM = pltpu.CompilerParams(vmem_limit_bytes=16 * MIB)
MOST = pltpu.CompilerParams(vmem_limit_bytes=49 * MIB)
FETCH = pltpu.CompilerParams(vmem_limit_bytes=58 * MIB)


def dot_nt(a, b):
    return lax.dot_general(a, b, (((1,), (1,)), ((), ())), preferred_element_type=F32)


def attention_kernel(
    owner_hbm,
    len_hbm,
    q_hbm,
    kn_hbm,
    vn_hbm,
    ck_hbm,
    cv_hbm,
    out_hbm,
    keep_ref,
    send_ref,
    owner_ref,
    len_ref,
    q_ref,
    kn_ref,
    vn_ref,
    ck_ref,
    cv_ref,
    out_ref,
    heads,
    sems,
):
    steps, rows, width = q_hbm.shape
    cached = ck_hbm.shape[1]
    groups = rows // GROUP
    fresh = [
        pltpu.make_async_copy(src, dst, sems.at[i])
        for i, (src, dst) in enumerate(
            ((q_hbm, q_ref), (kn_hbm, kn_ref), (vn_hbm, vn_ref), (out_hbm, out_ref))
        )
    ]
    small = [
        pltpu.make_async_copy(len_hbm, len_ref, sems.at[8]),
        pltpu.make_async_copy(owner_hbm, owner_ref, sems.at[9]),
    ]
    old = []
    for g in range(2):
        part = pl.ds(g * (rows // 2), rows // 2)
        for i, (src, dst) in enumerate(((ck_hbm, ck_ref), (cv_hbm, cv_ref))):
            sem = sems.at[4 + 2 * g + i]
            old.append(pltpu.make_async_copy(src.at[part], dst.at[part], sem))
    for copy in fresh[:3] + old[:1] + small + old[1:] + fresh[3:]:
        copy.start()
    parity = lax.axis_index("ep") % 2
    m = steps * GROUP
    n = GROUP * cached
    factor = 1.0 / math.sqrt(DH)
    row = lax.broadcasted_iota(jnp.int32, (m, n), 0)
    col = lax.broadcasted_iota(jnp.int32, (m, n), 1)
    own = col // cached == row % GROUP
    place = col % cached
    row = lax.broadcasted_iota(jnp.int32, (m, m), 0)
    col = lax.broadcasted_iota(jnp.int32, (m, m), 1)
    recent = (col % GROUP == row % GROUP) & (col // GROUP <= row // GROUP)
    row = lax.broadcasted_iota(jnp.int32, (m, rows), 0)
    col = lax.broadcasted_iota(jnp.int32, (m, rows), 1)
    for copy in fresh[:3] + small[:1]:
        copy.wait()
    lengths = len_ref[...].astype(F32)
    def score(g, h, live):
        part = slice(g * GROUP, (g + 1) * GROUP)
        cut = slice(h * DH, (h + 1) * DH)
        q = q_ref[:, part, cut].reshape(m, DH)
        so = dot_nt(q, ck_ref[part, :, cut].reshape(n, DH)) * factor
        sn = dot_nt(q, kn_ref[:, part, cut].reshape(m, DH)) * factor
        return jnp.where(live, so, NEVER), jnp.where(recent, sn, NEVER)

    def soften(so, sn):
        top = jnp.maximum(jnp.max(so, axis=1, keepdims=True), jnp.max(sn, axis=1, keepdims=True))
        eo = jnp.exp(so - top)
        en = jnp.exp(sn - top)
        total = jnp.sum(eo, axis=1, keepdims=True) + jnp.sum(en, axis=1, keepdims=True)
        return eo.astype(BF16), en.astype(BF16), 1.0 / total

    def gather(g, h, eo, en, inverse):
        part = slice(g * GROUP, (g + 1) * GROUP)
        cut = slice(h * DH, (h + 1) * DH)
        w = jnp.dot(
            eo, cv_ref[part, :, cut].reshape(n, DH), preferred_element_type=F32
        ) + jnp.dot(en, vn_ref[:, part, cut].reshape(m, DH), preferred_element_type=F32)
        return (w * inverse).astype(BF16).reshape(steps, GROUP, DH)

    scores = []
    for g in range(groups):
        if g % (groups // 2) == 0:
            for copy in old[g : g + 2]:
                copy.wait()
        length = jnp.sum(
            jnp.where(col == row % GROUP + g * GROUP, lengths, 0.0), axis=1, keepdims=True
        )
        live = own & (place < length.astype(jnp.int32))
        scores += [(g, h, *score(g, h, live)) for h in range(width // DH)]
    soft = [(g, h, *soften(so, sn)) for g, h, so, sn in scores]
    for g, h, *rest in soft:
        part = slice(g * GROUP, (g + 1) * GROUP)
        heads[:, part, h * DH : (h + 1) * DH] = gather(g, h, *rest)
    every = steps * rows
    half = every // 2
    mine = keep_ref.shape[1]
    own_rows = mine // steps
    j = lax.broadcasted_iota(jnp.int32, (every, 1), 0)
    core = jnp.where(j < half, parity, 1 - parity)
    chip = (j % half) // mine
    step = (j % mine) // own_rows
    wanted = step * rows + (chip * 2 + core) * own_rows + j % own_rows
    source = lax.broadcasted_iota(jnp.int32, (every, every), 1)
    order = jnp.where(source == wanted, 1.0, 0.0).astype(BF16)
    h = jnp.dot(order, heads[...].reshape(every, width), preferred_element_type=F32)
    h = h.astype(BF16)
    small[1].wait()
    rank = lax.axis_index("rep")
    bucket = jnp.int32(0)
    for b in range(owner_ref.shape[1]):
        bucket = jnp.where(owner_ref[0, b] == rank, b, bucket)
    fresh[3].wait()
    block = out_ref.shape[1]
    chips = half // mine
    for side, ref in enumerate((keep_ref, send_ref)):
        part = jnp.dot(
            h[side * half : (side + 1) * half], out_ref[...], preferred_element_type=F32
        )
        ref[:, :, :block] = part.astype(BF16).reshape(chips, mine, block)
        lane = lax.broadcasted_iota(jnp.int32, (chips, mine, ref.shape[2] - block), 2)
        ref[:, :, block:] = jnp.where(lane == side, bucket, 0).astype(F32).astype(BF16)


def attention(owner, queries, new_keys, new_values, cache_keys, cache_values, lengths, out, chips):
    steps, rows, width = queries.shape
    mine = steps * rows // (2 * chips)
    shape = (chips, mine, out.shape[1] + 128)
    vm = pl.BlockSpec(memory_space=VMEM)
    hbm = pl.BlockSpec(memory_space=pltpu.HBM)
    operands = (queries, new_keys, new_values, cache_keys, cache_values, out)
    return pl.pallas_call(
        attention_kernel,
        in_specs=[hbm] * (2 + len(operands)),
        out_specs=[vm, vm],
        out_shape=[jax.ShapeDtypeStruct(shape, BF16)] * 2,
        scratch_shapes=[SMEM(owner.shape, jnp.int32), VMEM(lengths.shape, jnp.int32)]
        + [VMEM(x.shape, BF16) for x in operands]
        + [
            VMEM((steps, rows, width), BF16),
            pltpu.SemaphoreType.DMA((10,)),
        ],
        compiler_params=FETCH,
        name="attention",
    )(owner, lengths, *operands)


def select_kernel(bucket_any, res_ref, gain_ref, out_ref, norm, bucket_ref, sem):
    fetch_buckets = pltpu.make_async_copy(bucket_any, bucket_ref, sem)
    fetch_buckets.start()
    blocks, rows, block = res_ref.shape
    total = jnp.zeros((rows, block), F32)
    for b in range(blocks):
        x = res_ref[b].astype(F32)
        total = total + x * x
    mean = jnp.sum(total, axis=1, keepdims=True) / (blocks * block)
    scale = lax.rsqrt(mean + EPSILON)
    for b in range(blocks):
        gain = gain_ref[:, b * block : (b + 1) * block]
        norm[b] = (res_ref[b].astype(F32) * scale * gain).astype(BF16)
    fetch_buckets.wait()
    for c in range(out_ref.shape[0]):
        out_ref[c] = norm[bucket_ref[c]]


def select(buckets, residual, gain):
    blocks, rows, block = residual.shape
    chips = buckets.shape[0]
    vm = pl.BlockSpec(memory_space=VMEM)
    return pl.pallas_call(
        select_kernel,
        in_specs=[pl.BlockSpec(memory_space=pl.ANY), vm, vm],
        out_specs=vm,
        out_shape=jax.ShapeDtypeStruct((chips, rows, block), BF16),
        scratch_shapes=[
            VMEM(residual.shape, BF16),
            SMEM(buckets.shape, jnp.int32),
            pltpu.SemaphoreType.DMA,
        ],
        compiler_params=ROOM,
        name="select",
    )(buckets, residual, gain)


def fetch_kernel(w_hbm, out_ref, sem):
    copy = pltpu.make_async_copy(w_hbm.at[pl.ds(0, out_ref.shape[0])], out_ref, sem)
    copy.start()
    copy.wait()


def fetch(weight, count):
    return pl.pallas_call(
        fetch_kernel,
        in_specs=[pl.BlockSpec(memory_space=pltpu.HBM)],
        out_specs=pl.BlockSpec(memory_space=VMEM),
        out_shape=jax.ShapeDtypeStruct((count,) + weight.shape[1:], BF16),
        scratch_shapes=[pltpu.SemaphoreType.DMA],
        compiler_params=MOST,
        name="fetch",
    )(weight)


def gate_up_kernel(x_ref, w_ref, out_ref):
    hidden = w_ref.shape[2]
    tile = 256
    for i in range(2):
        for j in range(0, hidden, tile):
            part = jnp.dot(x_ref[...], w_ref[i, :, j : j + tile], preferred_element_type=F32)
            out_ref[:, i * hidden + j : i * hidden + j + tile] = part.astype(BF16)


def gate_up(x, weight):
    vm = pl.BlockSpec(memory_space=VMEM)
    return pl.pallas_call(
        gate_up_kernel,
        in_specs=[vm, vm],
        out_specs=vm,
        out_shape=jax.ShapeDtypeStruct((x.shape[0], 2 * weight.shape[2]), BF16),
        compiler_params=ROOM,
        name="gate_up",
    )(x, weight)


def down_kernel(x_ref, w_ref, out_ref):
    width = w_ref.shape[1]
    for j in range(0, width, 256):
        part = slice(j, min(j + 256, width))
        out_ref[:, part] = dot_nt(x_ref[...], w_ref[2, part]).astype(BF16)


def down(x, weight):
    vm = pl.BlockSpec(memory_space=VMEM)
    return pl.pallas_call(
        down_kernel,
        in_specs=[vm, vm],
        out_specs=vm,
        out_shape=jax.ShapeDtypeStruct((x.shape[0], weight.shape[1]), BF16),
        compiler_params=ROOM,
        name="down",
    )(x, weight)


def combine_kernel(side, bucket_any, ids_ref, logits_ref, part_ref, *rest):
    *given, bucket_ref, sem = rest
    fetch_buckets = pltpu.make_async_copy(bucket_any, bucket_ref, sem)
    fetch_buckets.start()
    chips, rows, block = part_ref.shape
    steps = ids_ref.shape[0]
    ids = jnp.concatenate([ids_ref[t] for t in range(steps)], axis=0)
    logits = jnp.concatenate([logits_ref[t] for t in range(steps)], axis=0)
    affinity = 1.0 / (1.0 + jnp.exp(-logits))
    weight = ROUTE_SCALE * affinity / jnp.sum(affinity, axis=1, keepdims=True)
    parity = lax.axis_index("ep") % 2
    core = parity if side == 0 else 1 - parity
    expert = 2 * lax.broadcasted_iota(jnp.int32, (rows, chips), 1) + core
    share = jnp.zeros((rows, chips), F32)
    for k in range(ids.shape[1]):
        share = share + jnp.where(ids[:, k : k + 1] == expert, weight[:, k : k + 1], 0.0)
    if side == 0:
        (acc,) = given
        acc[...] = jnp.zeros_like(acc)
    else:
        start_ref, low_ref, high_ref, acc = given
        acc[...] = start_ref[...]
    fetch_buckets.wait()
    for c in range(chips):
        b = bucket_ref[side * chips + c]
        acc[b] = acc[b] + share[:, c : c + 1] * part_ref[c].astype(F32)
    if side == 1:
        half = low_ref.shape[0]
        low_ref[...] = acc[:half].astype(BF16)
        high_ref[...] = acc[half:].astype(BF16)


def combine(buckets, ids, logits, part, ranks, start=None):
    _, rows, block = part.shape
    vm = pl.BlockSpec(memory_space=VMEM)
    shape = (ranks, rows, block)
    small = [SMEM(buckets.shape, jnp.int32), pltpu.SemaphoreType.DMA]
    if start is None:
        side, operands, scratch = 0, (ids, logits, part), small
        out_shape = [jax.ShapeDtypeStruct(shape, F32)]
    else:
        side, operands, scratch = 1, (ids, logits, part, start), [VMEM(shape, F32)] + small
        out_shape = [jax.ShapeDtypeStruct((ranks // 2, rows, block), BF16)] * 2
    return pl.pallas_call(
        functools.partial(combine_kernel, side),
        in_specs=[pl.BlockSpec(memory_space=pl.ANY)] + [vm] * len(operands),
        out_specs=[vm] * len(out_shape),
        out_shape=out_shape,
        scratch_shapes=scratch,
        compiler_params=ROOM,
        name="combine",
    )(buckets, *operands)


def finish_kernel(low_ref, high_ref, res_ref, out_ref):
    half, rows, block = low_ref.shape
    own = out_ref.shape[1]
    for b in range(2 * half):
        part = low_ref[b] if b < half else high_ref[b - half]
        x = res_ref[b].astype(F32)[:rows] + part.astype(F32)
        for t in range(out_ref.shape[0]):
            row = x[t * own : (t + 1) * own].astype(BF16)
            out_ref[t, :, b * block : (b + 1) * block] = row


def finish(low, high, residual, steps, own):
    blocks, _, block = residual.shape
    vm = pl.BlockSpec(memory_space=VMEM)
    return pl.pallas_call(
        finish_kernel,
        in_specs=[vm, vm, vm],
        out_specs=vm,
        out_shape=jax.ShapeDtypeStruct((steps, own, blocks * block), BF16),
        compiler_params=ROOM,
        name="finish",
    )(low, high, residual)


def on_device(
    hidden_in,
    queries,
    new_keys,
    new_values,
    cache_keys,
    cache_values,
    cache_lengths,
    expert_ids,
    router_logits,
    norm_gain,
    out_sectioned,
    expert_sectioned,
    bucket_owner,
):
    steps, own_rows, width = hidden_in.shape
    n_ep = lax.axis_size("ep")
    n_rep = lax.axis_size("rep")
    chips = n_ep // 2
    block = width // n_rep
    mine = own_rows * steps
    rank = lax.axis_index("rep")
    pair = [(j, j ^ 1) for j in range(n_ep)]
    cores = [[j for j in range(n_ep) if j % 2 == k] for k in range(2)]

    def swap(x):
        return lax.ppermute(x, "ep", pair)

    def across(x):
        return lax.all_to_all(x, "ep", 0, 0, tiled=True, axis_index_groups=cores)

    def over_rep(x):
        return lax.all_to_all(x, "rep", 0, 0, tiled=True)

    keep, send = attention(
        bucket_owner,
        queries,
        new_keys,
        new_values,
        cache_keys,
        cache_values,
        cache_lengths[None],
        out_sectioned,
        chips,
    )
    own_block = lax.dynamic_slice_in_dim(hidden_in, rank * block, block, 2).reshape(mine, block)
    both = (keep.astype(F32) + swap(send).astype(F32)).astype(BF16)
    both, own_block = lax.optimization_barrier((both, own_block))
    parts = across(both)
    buckets = parts[:, 0, block : block + 2].astype(jnp.int32).T
    own_buckets, buckets = buckets[0], buckets.reshape(-1)
    residual = jnp.sum(parts[:, :, :block].astype(F32), axis=0) + own_block.astype(F32)
    residual = residual.astype(BF16)
    weight = jnp.transpose(expert_sectioned[0], (1, 0, 2))
    residual, weight = lax.optimization_barrier((residual, weight))
    other = swap(residual)
    into = fetch(weight, 2)
    other, into, own_buckets, buckets = lax.optimization_barrier(
        (other, into, own_buckets, buckets)
    )
    residual = jnp.concatenate([residual, other], axis=0)
    residual = over_rep(jnp.broadcast_to(residual, (n_rep,) + residual.shape))
    chosen = select(own_buckets, residual, norm_gain.reshape(1, width))
    arrivals = across(chosen).reshape(-1, block)
    hidden = weight.shape[2]
    partial = gate_up(arrivals, into)
    partial = over_rep(partial.reshape(n_rep, -1, 2 * hidden))
    partial = jnp.sum(partial.astype(F32), axis=0)
    activated = (jax.nn.silu(partial[:, :hidden]) * partial[:, hidden:]).astype(BF16)
    activated = over_rep(jnp.broadcast_to(activated, (n_rep,) + activated.shape))
    result = down(activated.reshape(-1, hidden), weight)
    back = across(result.reshape(chips, 2 * mine, block))
    got = swap(back[:, mine:])
    (start,) = combine(buckets, expert_ids, router_logits, back[:, :mine], n_rep)
    low, high = combine(buckets, expert_ids, router_logits, got, n_rep, start)
    lines = n_rep // 2
    turns = (
        [(j, j ^ 1) for j in range(n_rep)],
        [(j, j ^ 2) for j in range(n_rep)],
        [(j, ((j // 2 + (1 if j // 2 % 2 else -1)) % lines) * 2 + j % 2) for j in range(n_rep)],
    )
    def add(x, turn):
        return (x.astype(F32) + lax.ppermute(x, "rep", turn).astype(F32)).astype(BF16)

    for i in range(3):
        low, high = add(low, turns[i]), add(high, turns[(i + 1) % 3])
    return finish(low, high, residual, steps, own_rows)


def solution(mesh):
    return jax.shard_map(
        on_device,
        mesh=mesh,
        in_specs=(
            P(None, "ep", None),
            P(None, None, "ep"),
            P(None, None, "ep"),
            P(None, None, "ep"),
            P(None, None, "ep"),
            P(None, None, "ep"),
            P(),
            P(None, "ep", None),
            P(None, "ep", None),
            P(),
            P("ep", "rep"),
            P("ep", "rep", None, None),
            P("ep", None),
        ),
        out_specs=P(None, "ep", None),
        check_vma=False,
    )
```
